256 devices in a mesh: grp: 4 (over y), tile: 64 (over z, x, core).
Axes of the slice: x: 4, y: 4, z: 8, core: 2. Of those that a mesh axis runs over, the one named last changes fastest.
Arguments:
- pieces: bfloat16 [16384, 128, 128], P(('grp', 'tile')), may hold values from -6 to 6
- row_taps: bfloat16 [21, 41], replicated, may hold values from -1 to 1
- col_taps: bfloat16 [21, 41], replicated, may hold values from -1 to 1
- coeffs: float32 [16384, 21], P(('grp', 'tile')), may hold values from -1.25 to 1.25
- weights: bfloat16 [16384], P(('grp', 'tile')), may hold values from 0.25 to 4
- blocks: int32 [16384], P(('grp', 'tile')), may hold values from 0 to 15
- routes: int32 [16384, 1], P(('grp', 'tile')), may hold values from 0 to 63; in each aligned block of 64 rows (0 to 63, 64 to 127, ...) at most 2 rows name the same one
Outputs:
- difference: bfloat16 [16384, 128, 128], P(('grp', 'tile'))
- coadd: bfloat16 [1024, 16384], P('tile')
The draws below stay inside these ranges and needn't reach their ends.
Inputs may be any that keep to these rules, and one draw needn't show every extreme that they name: `routes`: in the rows of one device no owner is named more than 2 times, a bound that some block reaches.
All inputs are finite; a program needn't handle non-finite values.
Results may differ from the reference program's by a relative error of at most 0.0059.
Values may be sent and summed in bfloat16 or wider, within the bound.
No kernel may reach another device: no remote copies, remote signals or barrier semaphores. Data moves between devices by JAX's collectives and lax.ppermute only.
A program may use at most 64 MiB of HBM per device.

```python
import math
import jax
import jax.numpy as jnp
import numpy as np
from jax import lax

PIX = 128
KW = 41
NB = 21
BLOCKS = 16
PIECES = 64
CAP = 2
ALLPIECES = 16384
PATCHROWS = 1024
N_TILE = 64


def set_ends(entries, key, low, high):
    longest = entries.shape.index(max(entries.shape))
    spots = []
    for shift in (0, 1):
        where = [jax.random.randint(jax.random.fold_in(key, axis), (), 0, length) for axis, length in enumerate(entries.shape)]
        where[longest] = (where[longest] + shift) % entries.shape[longest]
        spots.append(tuple(where))
    return entries.at[spots[0]].set(low).at[spots[1]].set(high)


def block_levels(rng, shape, cuts, least, largest):
    def one(dim, blocks):
        draws = jax.random.uniform(jax.random.fold_in(jax.random.fold_in(rng, 6), dim), (blocks,), jnp.float32, least / len(cuts), largest / len(cuts))
        return jnp.repeat(jnp.exp(draws), shape[dim] // blocks).reshape((-1,) + (1,) * (len(shape) - dim - 1))

    gain = one(*cuts[0])
    for cut in cuts[1:]:
        gain = gain * one(*cut)
    return gain


def routed_block(stream_key, own, number, rows, amount, top, limit, skew):
    sequence = jax.random.permutation(stream_key, amount)
    packed, usual = portions_of(amount, rows * top, limit, skew, True), portions_of(amount, rows * top, limit, skew, False)
    places = jnp.arange(amount)

    def named(tallies, offset_by):
        used = int((tallies > 0).sum())
        fixed = max(1, used // 4)
        shifted = fixed + (places - fixed + offset_by * (used - fixed)) % max(1, amount - fixed)
        return jnp.zeros((amount,), jnp.int32).at[sequence[jnp.where(places < fixed, places, shifted)]].set(jnp.asarray(tallies, jnp.int32))

    tallies = jnp.where(number % 4 == 0, named(packed, number // 4), named(usual, number - number // 4 - 1))
    mixed = jax.random.permutation(jax.random.fold_in(own, 3), amount)
    donor, sink = mixed[0:amount // 2 * 2:2], mixed[1:amount // 2 * 2:2]
    room = jnp.minimum(tallies[donor] - 1, limit - tallies[sink]) // 2
    room = jnp.where((donor == sequence[0]) | (sink == sequence[0]) | (tallies[sink] == 0), 0, jnp.maximum(room, 0))
    shifted = jax.random.randint(jax.random.fold_in(own, 4), (amount // 2,), 0, 1 << 20) % (room + 1)
    tallies = tallies.at[donor].add(-shifted).at[sink].add(shifted)
    members = jnp.searchsorted(jnp.cumsum(tallies), jnp.arange(rows * top), side="right").astype(jnp.int32)
    table = members.reshape(top, rows).T
    table = table[jax.random.permutation(jax.random.fold_in(own, 1), rows)]
    offset_by = jax.random.randint(jax.random.fold_in(own, 2), (rows, 1), 0, top)
    return jnp.take_along_axis(table, (jnp.arange(top)[None, :] + offset_by) % top, axis=1)


def portions_of(count, total, limit, skew, full):
    weights = [(1 << 20) // math.isqrt(rank ** skew) + 1 for rank in range(1, count + 1)]
    largest = limit if full else min(limit, max(-(-total // count), total * weights[0] // sum(weights)))
    least = 1 if total - largest >= count - 1 else 0
    given, rest = [largest] + [least] * (count - 1), total - largest - least * (count - 1)
    while rest > 0:
        free = [i for i in range(1, count) if given[i] < largest] or [i for i in range(1, count) if given[i] < limit]
        mass, remaining = sum([weights[i] for i in free]), rest
        for i in free:
            more = min(limit - given[i], max(1, remaining * weights[i] // mass), rest)
            given[i] = given[i] + more
            rest = rest - more
    return np.array(given)


def noise(key, dims, spread, limit, shards=(), kind=jnp.bfloat16):
    level = block_levels(key, dims, shards, -0.22, 0.18) if shards else 1.0
    result = jax.random.normal(key, dims, jnp.float32) * spread * level
    return jnp.minimum(jnp.maximum(result, -limit), limit).astype(kind)


def setup_inputs(seed: int = 0) -> dict:
    streams_of = jax.random.split(jax.random.key(seed), 8)
    pieces = noise(streams_of[0], (ALLPIECES, PIX, PIX), 1.0, 6.0, ((0, 256),))
    row_taps = noise(streams_of[1], (NB, KW), KW ** -0.5, 1.0)
    col_taps = noise(streams_of[2], (NB, KW), KW ** -0.5, 1.0)
    coeffs = noise(streams_of[3], (ALLPIECES, NB), NB ** -0.5, 1.25, ((0, 256),), jnp.float32)
    weights = jnp.clip(jnp.exp(math.log(4.0) - 2.7725887 * jax.random.uniform(streams_of[4], (ALLPIECES,), jnp.float32) ** block_levels(streams_of[4], (ALLPIECES,), ((0, 256),), -0.2, 0.2)), 0.25, 4.0).astype(jnp.bfloat16)
    blocks = set_ends(jax.random.randint(streams_of[5], (ALLPIECES,), 0, BLOCKS), jax.random.fold_in(streams_of[5], 1), 0, BLOCKS - 1).astype(jnp.int32)
    routes_keys = jax.random.split(jax.random.fold_in(streams_of[6], 1), ALLPIECES // PIECES)
    routes_turns = jax.random.permutation(jax.random.fold_in(streams_of[6], 3), ALLPIECES // PIECES)
    routes = jax.vmap(lambda own, number: routed_block(jax.random.fold_in(streams_of[6], 2), own, number, PIECES, N_TILE, 1, CAP, 2))(routes_keys, routes_turns).reshape((ALLPIECES, 1))
    return dict(pieces=pieces, row_taps=row_taps, col_taps=col_taps, coeffs=coeffs, weights=weights, blocks=blocks, routes=routes)


def toeplitz(taps, side):
    width = taps.shape[1]
    half = (width - 1) // 2
    rows = jnp.arange(side, dtype=jnp.int32)
    offset = rows[None, :] - rows[:, None] + half
    marks = (offset[:, :, None] == jnp.arange(width, dtype=jnp.int32)[None, None, :]).astype(jnp.float32)
    return jnp.einsum('imk,bk->bim', marks, taps.astype(jnp.float32)).astype(jnp.bfloat16)


def convolve_group(blocks_in, coef, row_mats, col_mats):
    inner = jnp.einsum('pim,bjm->pbij', blocks_in.astype(jnp.float32), col_mats.astype(jnp.float32))
    inner = (inner * coef[:, :, None, None]).astype(jnp.bfloat16)
    outer = jnp.einsum('bim,pbmj->pij', row_mats.astype(jnp.float32), inner.astype(jnp.float32))
    return outer.astype(jnp.bfloat16)


def reference(pieces, row_taps, col_taps, coeffs, weights, blocks, routes):
    side = pieces.shape[1]
    row_mats = toeplitz(row_taps, side)
    col_mats = toeplitz(col_taps, side)
    total = pieces.shape[0]
    group = min(8, total)
    grouped = pieces.reshape(total // group, group, side, side)
    coef_grouped = coeffs.reshape(total // group, group, coeffs.shape[1])
    matched = lax.map(lambda item: convolve_group(item[0], item[1], row_mats, col_mats), (grouped, coef_grouped))
    matched = matched.reshape(total, side * side)
    target = (routes[:, 0] * BLOCKS + blocks).astype(jnp.int32)
    weight_f = weights.astype(jnp.float32)
    numer = jax.ops.segment_sum(matched.astype(jnp.float32) * weight_f[:, None], target, num_segments=PATCHROWS)
    wsum = jax.ops.segment_sum(weight_f, target, num_segments=PATCHROWS)
    coadd = (numer / jnp.maximum(wsum, 1.0)[:, None]).astype(jnp.bfloat16)
    under = coadd[target]
    difference = (matched.astype(jnp.float32) - under.astype(jnp.float32)).astype(jnp.bfloat16)
    return difference.reshape(total, side, side), coadd
```

```python
import functools

import jax
import jax.numpy as jnp
from jax import lax
from jax.experimental import pallas as pl
from jax.experimental.pallas import tpu as pltpu
from jax.sharding import Mesh, PartitionSpec as P

BLOCKS = 16
SIDE = 128
GROUP = 16
HEAD = 8
TAIL = 16
FAR = "far"
PLANE = ("y", "near", "x", "c")
EVERY = ("y", "far", "near", "x", "c")
BF16 = jnp.bfloat16
F32 = jnp.float32


def params(limit=56 << 20):
    return pltpu.CompilerParams(vmem_limit_bytes=limit)


def cost(flops, nbytes):
    return pl.CostEstimate(flops=flops, bytes_accessed=nbytes, transcendentals=0)


def band(taps_ref, b, half):
    line = jnp.broadcast_to(taps_ref[b : b + 1, :], (SIDE, SIDE))
    moved = pltpu.roll(line, 0, 1, stride=1, stride_axis=0)
    rows = lax.broadcasted_iota(jnp.int32, (SIDE, SIDE), 0)
    columns = lax.broadcasted_iota(jnp.int32, (SIDE, SIDE), 1)
    return jnp.where(jnp.abs(columns - rows) <= half, moved, 0.0)


def conv_kernel(nb, half, coef_ref, x_ref, col_taps_ref, row_taps_ref, out_ref, col_ref, row_ref, taps_ref, z_ref, m_ref):
    step = pl.program_id(0)

    @pl.when(step == 0)
    def _():
        for source, target, flip in ((col_taps_ref, col_ref, True), (row_taps_ref, row_ref, False)):
            taps_ref[...] = jnp.zeros_like(taps_ref)
            taps_ref[:nb, : 2 * half + 1] = source[...].astype(F32)
            taps_ref[...] = pltpu.roll(taps_ref[...], SIDE - half, 1)
            for b in range(nb):
                matrix = band(taps_ref, b, half)
                matrix = matrix.T if flip else matrix
                target[:, b * SIDE : (b + 1) * SIDE] = matrix.astype(BF16)

    x = x_ref[...].reshape(GROUP * SIDE, SIDE)
    for first in range(0, nb, 2):
        some = min(2, nb - first)
        inner = jnp.dot(x, col_ref[:, first * SIDE : (first + some) * SIDE], preferred_element_type=F32)
        for k in range(some):
            b = first + k
            for p in range(GROUP):
                part = inner[p * SIDE : (p + 1) * SIDE, k * SIDE : (k + 1) * SIDE]
                z_ref[p // 2, b * SIDE : (b + 1) * SIDE, (p % 2) * SIDE : (p % 2 + 1) * SIDE] = (
                    part * coef_ref[step * GROUP + p, b]
                ).astype(BF16)
    for pair in range(GROUP // 2):
        outer = jnp.dot(row_ref[...], z_ref[pair], preferred_element_type=F32)
        m_ref[2 * pair * SIDE : (2 * pair + 1) * SIDE] = outer[:, :SIDE]
        m_ref[(2 * pair + 1) * SIDE : (2 * pair + 2) * SIDE] = outer[:, SIDE:]
    per = SIDE // out_ref.shape[0]
    for i in range(SIDE):
        t, k = divmod(i, per)
        out_ref[t, :, k * SIDE : (k + 1) * SIDE] = m_ref[pl.ds(i, GROUP, stride=SIDE), :].astype(BF16)


def convolve(pieces, coeffs, col_taps, row_taps, chunks):
    count = pieces.shape[0]
    nb, width = row_taps.shape
    padded = -(-nb // 8) * 8
    return pl.pallas_call(
        functools.partial(conv_kernel, nb, (width - 1) // 2),
        grid=(count // GROUP,),
        in_specs=[
            pl.BlockSpec(memory_space=pltpu.SMEM),
            pl.BlockSpec((GROUP, SIDE, SIDE), lambda g: (g, 0, 0)),
            pl.BlockSpec((nb, width), lambda g: (0, 0)),
            pl.BlockSpec((nb, width), lambda g: (0, 0)),
        ],
        out_specs=pl.BlockSpec((chunks, GROUP, SIDE * SIDE // chunks), lambda g: (0, g, 0)),
        out_shape=jax.ShapeDtypeStruct((chunks, count, SIDE * SIDE // chunks), BF16),
        scratch_shapes=[
            pltpu.VMEM((SIDE, nb * SIDE), BF16),
            pltpu.VMEM((SIDE, nb * SIDE), BF16),
            pltpu.VMEM((padded, SIDE), F32),
            pltpu.VMEM((GROUP // 2, nb * SIDE, 2 * SIDE), BF16),
            pltpu.VMEM((GROUP * SIDE, SIDE), F32),
        ],
        compiler_params=params(),
        cost_estimate=cost(count * nb * SIDE**3 * 4, count * SIDE * SIDE * 4),
        name="convolve",
    )(coeffs, pieces, col_taps, row_taps)


def partial_kernel(steps, own_rows, z_ref, info_ref, got_ref, *refs):
    outs, (row_ref, weight_ref) = refs[:steps], refs[steps:]
    sources = info_ref.shape[0]
    left = lax.broadcasted_iota(jnp.int32, (1, SIDE), 1) < SIDE // 2
    for a in range(sources // 2):
        for line, target in ((0, row_ref), (1, weight_ref)):
            both = jnp.where(left, info_ref[2 * a, line : line + 1, :], info_ref[2 * a + 1, line : line + 1, :])
            target[:, a * SIDE : (a + 1) * SIDE] = both
    row = row_ref[...].astype(jnp.int32)
    weight = weight_ref[...]
    index = lax.broadcasted_iota(jnp.int32, (own_rows, row.shape[1]), 0)
    for k in range(steps):
        first = lax.rem(z_ref[0] + k, steps) * own_rows
        marks = jnp.where(index == row - first, weight, 0.0)
        part = jnp.dot(marks.astype(BF16), got_ref[...], preferred_element_type=F32)
        outs[k][:own_rows, :] = part.astype(BF16)
        total = jnp.broadcast_to(jnp.sum(marks, axis=1, keepdims=True), (own_rows, SIDE)).T[:TAIL]
        high = total.astype(BF16).astype(F32)
        middle = (total - high).astype(BF16).astype(F32)
        low = total - high - middle
        line = lax.broadcasted_iota(jnp.int32, total.shape, 0)
        terms = jnp.where(line == 0, high, jnp.where(line == 1, middle, jnp.where(line == 2, low, 0.0)))
        outs[k][own_rows:, :] = terms.astype(BF16)


def partial_sums(z, info, got, steps, own_rows):
    held, width = got.shape
    vmem = pl.BlockSpec(memory_space=pltpu.VMEM)
    return pl.pallas_call(
        functools.partial(partial_kernel, steps, own_rows),
        in_specs=[pl.BlockSpec(memory_space=pltpu.SMEM), vmem, vmem],
        out_specs=[vmem] * steps,
        out_shape=[jax.ShapeDtypeStruct((own_rows + TAIL, width), BF16)] * steps,
        scratch_shapes=[pltpu.VMEM((1, held), F32), pltpu.VMEM((1, held), F32)],
        compiler_params=params(),
        cost_estimate=cost(2 * steps * own_rows * held * width, (held + steps * own_rows) * width * 2),
        name="partial_sums",
    )(z, info, got)


def average_kernel(own_rows, *refs):
    parts, out_ref = refs[:-1], refs[-1]
    terms = sum(ref[own_rows:, :].astype(F32) for ref in parts)
    line = jnp.sum(terms, axis=0, keepdims=True)
    below = jnp.maximum(jnp.broadcast_to(line, (SIDE, own_rows)).T, 1.0)
    total = sum(ref[:own_rows, :].astype(F32) for ref in parts)
    for k in range(total.shape[1] // SIDE):
        span = slice(k * SIDE, (k + 1) * SIDE)
        out_ref[:, span] = (total[:, span] / below).astype(BF16)


def average(parts, own_rows):
    width = parts[0].shape[1]
    vmem = pl.BlockSpec(memory_space=pltpu.VMEM)
    return pl.pallas_call(
        functools.partial(average_kernel, own_rows),
        in_specs=[vmem] * len(parts),
        out_specs=vmem,
        out_shape=jax.ShapeDtypeStruct((own_rows, width), BF16),
        compiler_params=params(),
        cost_estimate=cost(10 * own_rows * width, 18 * own_rows * width),
        name="average",
    )(*parts)


def subtract_kernel(count, groups, z_ref, info_ref, got_ref, *refs):
    coadds, out_ref, all_ref = refs[:-2], refs[-2], refs[-1]
    steps, own_rows = len(coadds), coadds[0].shape[0]
    total_rows = steps * own_rows
    for k in range(steps):
        all_ref[k * own_rows : (k + 1) * own_rows, :] = coadds[k][...]
    sources = out_ref.shape[0]
    left = lax.broadcasted_iota(jnp.int32, (1, SIDE), 1) < SIDE // 2
    index = lax.broadcasted_iota(jnp.int32, (SIDE, total_rows), 1).astype(F32)
    lanes = min(4, sources // 2)
    for first in range(0, sources // 2, lanes):
        marks = []
        for a in range(first, first + lanes):
            row = jnp.where(left, info_ref[2 * a, :1, :], info_ref[2 * a + 1, :1, :]).astype(jnp.int32)
            back = jnp.bitwise_and(z_ref[0] - jnp.right_shift(row, own_rows.bit_length() - 1) + steps, steps - 1)
            row = back * own_rows + jnp.bitwise_and(row, own_rows - 1)
            column = jnp.broadcast_to(row.astype(F32), (SIDE, SIDE)).T
            column = jnp.concatenate([column] * (total_rows // SIDE), axis=1)
            marks.append(jnp.where(index == column, 1.0, 0.0).astype(BF16))
        under = jnp.dot(jnp.concatenate(marks), all_ref[...], preferred_element_type=F32)
        for a in range(2 * lanes):
            s = 2 * first + a
            piece = got_ref[s * count : (s + 1) * count, :].astype(F32)
            out_ref[s, :count, :] = (piece - under[a * count : (a + 1) * count]).astype(BF16)
            k = s % groups
            out_ref[s, count:, :] = coadds[0][k * BLOCKS : (k + 1) * BLOCKS, :]


def subtract(z, info, got, coadds, count, groups):
    held, width = got.shape
    sources = held // count
    steps, own_rows = len(coadds), coadds[0].shape[0]
    vmem = pl.BlockSpec(memory_space=pltpu.VMEM)
    return pl.pallas_call(
        functools.partial(subtract_kernel, count, groups),
        in_specs=[pl.BlockSpec(memory_space=pltpu.SMEM)] + [vmem] * (2 + steps),
        out_specs=vmem,
        out_shape=jax.ShapeDtypeStruct((sources, count + BLOCKS, width), BF16),
        scratch_shapes=[pltpu.VMEM((steps * own_rows, width), BF16)],
        compiler_params=params(),
        cost_estimate=cost(2 * steps * own_rows * held * width, (2 * held + steps * own_rows) * width * 2),
        name="subtract",
    )(z, info, got, *coadds)


def place_kernel(back_ref, coadd_ref, diff_ref, template_ref, m_ref):
    chunks, _, width = back_ref.shape
    per = width // SIDE
    for t in range(chunks):
        for k in range(per):
            m_ref[pl.ds(t * per + k, GROUP, stride=SIDE), :] = back_ref[
                t, :, k * SIDE : (k + 1) * SIDE
            ].astype(F32)
    diff_ref[...] = m_ref[...].astype(BF16).reshape(diff_ref.shape)
    for t in range(coadd_ref.shape[0]):
        template_ref[:, t * width : (t + 1) * width] = coadd_ref[t]


def place(back, count):
    chunks, _, width = back.shape
    steps = count // GROUP
    some = chunks // steps
    return pl.pallas_call(
        place_kernel,
        grid=(steps,),
        in_specs=[
            pl.BlockSpec((chunks, GROUP, width), lambda g: (0, g, 0)),
            pl.BlockSpec((some, BLOCKS, width), lambda g: (g, count // BLOCKS, 0)),
        ],
        out_specs=(
            pl.BlockSpec((GROUP, SIDE, SIDE), lambda g: (g, 0, 0)),
            pl.BlockSpec((BLOCKS, some * width), lambda g: (0, g)),
        ),
        out_shape=(
            jax.ShapeDtypeStruct((count, SIDE, SIDE), BF16),
            jax.ShapeDtypeStruct((BLOCKS, SIDE * SIDE), BF16),
        ),
        scratch_shapes=[pltpu.VMEM((GROUP * SIDE, SIDE), F32)],
        compiler_params=params(),
        cost_estimate=cost(0, 4 * count * SIDE * SIDE),
        name="place",
    )(back, back)


def shift(array, by, steps):
    return lax.ppermute(array, FAR, [(i, (i + by) % steps) for i in range(steps)])


def body(pieces, row_taps, col_taps, coeffs, weights, blocks, routes):
    count = pieces.shape[0]
    steps = lax.axis_size(FAR)
    chunks = lax.axis_size(PLANE)
    groups = chunks // lax.axis_size("y")
    own_rows = groups * BLOCKS
    z = lax.axis_index(FAR).astype(jnp.int32).reshape(1)

    row = (routes[:, 0] * BLOCKS + blocks).astype(F32)
    info = jnp.stack([jnp.tile(row, 2), jnp.tile(weights.astype(F32), 2)])
    info = jnp.pad(info, ((0, HEAD - 2), (0, 0)))
    info = jnp.broadcast_to(info, (chunks,) + info.shape)
    info = lax.all_to_all(info, PLANE, split_axis=0, concat_axis=0, tiled=True)

    sent = convolve(pieces, coeffs, col_taps, row_taps, chunks)
    got = lax.all_to_all(sent, PLANE, split_axis=0, concat_axis=0, tiled=True)
    got = got.reshape(chunks * count, -1)
    sums = partial_sums(z, info, got, steps, own_rows)
    own = average([sums[0]] + [shift(sums[k], k, steps) for k in range(1, steps)], own_rows)
    coadds = [own] + [shift(own, k, steps) for k in range(1, steps)]
    back = subtract(z, info, got, coadds, count, groups)
    back = lax.all_to_all(back, PLANE, split_axis=0, concat_axis=0, tiled=True)
    return place(back, count)


def solution(mesh):
    finer = Mesh(mesh.devices.reshape(4, 4, 2, 4, 2), EVERY)
    in_specs = (
        P(EVERY, None, None),
        P(),
        P(),
        P(EVERY, None),
        P(EVERY),
        P(EVERY),
        P(EVERY, None),
    )
    out_specs = (P(EVERY, None, None), P(EVERY[1:], None))
    return jax.shard_map(body, mesh=finer, in_specs=in_specs, out_specs=out_specs, check_vma=False)
```

```python
import functools

import jax
import jax.numpy as jnp
from jax import lax
from jax.experimental import pallas as pl
from jax.experimental.pallas import tpu as pltpu
from jax.sharding import Mesh, PartitionSpec as P

BLOCKS = 16
SIDE = 128
GROUP = 16
HEAD = 8
TAIL = 16
STRIDE = 132
FAR = "far"
PLANE = ("c", "x", "near", "y")
EVERY = ("y", "far", "near", "x", "c")
BF16 = jnp.bfloat16
F32 = jnp.float32


def params(limit=63 << 20):
    return pltpu.CompilerParams(vmem_limit_bytes=limit)


def cost(flops, nbytes):
    return pl.CostEstimate(flops=flops, bytes_accessed=nbytes, transcendentals=0)


def band(taps_ref, b, half):
    line = jnp.broadcast_to(taps_ref[b : b + 1, :], (SIDE, SIDE))
    moved = pltpu.roll(line, 0, 1, stride=1, stride_axis=0)
    rows = lax.broadcasted_iota(jnp.int32, (SIDE, SIDE), 0)
    columns = lax.broadcasted_iota(jnp.int32, (SIDE, SIDE), 1)
    return jnp.where(jnp.abs(columns - rows) <= half, moved, 0.0)


def conv_kernel(nb, half, coef_ref, x_ref, col_taps_ref, row_taps_ref, out_ref, col_ref, row_ref, taps_ref, z_ref, m_ref):
    step = pl.program_id(0)

    @pl.when(step == 0)
    def _():
        for source, target, flip in ((col_taps_ref, col_ref, True), (row_taps_ref, row_ref, False)):
            taps_ref[...] = jnp.zeros_like(taps_ref)
            taps_ref[:nb, : 2 * half + 1] = source[...].astype(F32)
            taps_ref[...] = pltpu.roll(taps_ref[...], SIDE - half, 1)
            for b in range(nb):
                matrix = band(taps_ref, b, half)
                matrix = matrix.T if flip else matrix
                target[:, b * SIDE : (b + 1) * SIDE] = matrix.astype(BF16)

    x = x_ref[...].reshape(GROUP * SIDE, SIDE)
    for first in range(0, nb, 2):
        some = min(2, nb - first)
        inner = jnp.dot(x, col_ref[:, first * SIDE : (first + some) * SIDE], preferred_element_type=F32)
        for k in range(some):
            b = first + k
            for p in range(GROUP):
                part = inner[p * SIDE : (p + 1) * SIDE, k * SIDE : (k + 1) * SIDE]
                z_ref[p // 2, b * SIDE : (b + 1) * SIDE, (p % 2) * SIDE : (p % 2 + 1) * SIDE] = (
                    part * coef_ref[step * GROUP + p, b]
                ).astype(BF16)
    for pair in range(GROUP // 2):
        outer = jnp.dot(row_ref[...], z_ref[pair], preferred_element_type=F32)
        for h in range(2):
            at = (2 * pair + h) * STRIDE
            m_ref[at : at + SIDE] = outer[:, h * SIDE : (h + 1) * SIDE]
    per = SIDE // out_ref.shape[0]
    for i in range(SIDE):
        t, k = divmod(i, per)
        out_ref[t, :, k * SIDE : (k + 1) * SIDE] = m_ref[pl.ds(i, GROUP, stride=STRIDE), :].astype(BF16)


def convolve(pieces, coeffs, col_taps, row_taps, chunks):
    count = pieces.shape[0]
    nb, width = row_taps.shape
    padded = -(-nb // 8) * 8
    return pl.pallas_call(
        functools.partial(conv_kernel, nb, (width - 1) // 2),
        grid=(count // GROUP,),
        in_specs=[
            pl.BlockSpec(memory_space=pltpu.SMEM),
            pl.BlockSpec((GROUP, SIDE, SIDE), lambda g: (g, 0, 0)),
            pl.BlockSpec((nb, width), lambda g: (0, 0)),
            pl.BlockSpec((nb, width), lambda g: (0, 0)),
        ],
        out_specs=pl.BlockSpec((chunks, GROUP, SIDE * SIDE // chunks), lambda g: (0, g, 0)),
        out_shape=jax.ShapeDtypeStruct((chunks, count, SIDE * SIDE // chunks), BF16),
        scratch_shapes=[
            pltpu.VMEM((SIDE, nb * SIDE), BF16),
            pltpu.VMEM((SIDE, nb * SIDE), BF16),
            pltpu.VMEM((padded, SIDE), F32),
            pltpu.VMEM((GROUP // 2, nb * SIDE, 2 * SIDE), BF16),
            pltpu.VMEM((GROUP * STRIDE, SIDE), F32),
        ],
        compiler_params=params(),
        cost_estimate=cost(count * nb * SIDE**3 * 4, count * SIDE * SIDE * 4),
        name="convolve",
    )(coeffs, pieces, col_taps, row_taps)


def describe_kernel(steps, own_rows, z_ref, info_ref, line_ref, out_ref):
    sources = info_ref.shape[0]
    left = lax.broadcasted_iota(jnp.int32, (1, SIDE), 1) < SIDE // 2
    for a in range(sources // 2):
        span = slice(a * SIDE, (a + 1) * SIDE)
        for line in range(2):
            even = info_ref[2 * a, line : line + 1, :]
            odd = pltpu.roll(info_ref[2 * a + 1, line : line + 1, :], SIDE // 2, 1)
            line_ref[line : line + 1, span] = jnp.where(left, even, odd)
    row, weight = line_ref[:1, :].astype(jnp.int32), line_ref[1:2, :]
    index = lax.broadcasted_iota(jnp.int32, (own_rows, row.shape[1]), 0)
    for k in range(steps):
        first = lax.rem(z_ref[0] + k, steps) * own_rows
        marks = jnp.where(index == row - first, weight, 0.0)
        total = jnp.broadcast_to(jnp.sum(marks, axis=1, keepdims=True), (own_rows, SIDE))
        total = total.T[:TAIL]
        high = total.astype(BF16).astype(F32)
        middle = (total - high).astype(BF16).astype(F32)
        low = total - high - middle
        line = lax.broadcasted_iota(jnp.int32, total.shape, 0)
        terms = jnp.where(line == 0, high, jnp.where(line == 1, middle, jnp.where(line == 2, low, 0.0)))
        out_ref[k * TAIL : (k + 1) * TAIL, :] = terms.astype(BF16)


def describe(z, info, steps, own_rows):
    held = info.shape[0] * SIDE // 2
    vmem = pl.BlockSpec(memory_space=pltpu.VMEM)
    return pl.pallas_call(
        functools.partial(describe_kernel, steps, own_rows),
        in_specs=[pl.BlockSpec(memory_space=pltpu.SMEM), vmem],
        out_specs=[vmem] * 2,
        out_shape=[jax.ShapeDtypeStruct((HEAD, held), F32)]
        + [jax.ShapeDtypeStruct((steps * TAIL, own_rows), BF16)],
        compiler_params=params(),
        cost_estimate=cost(4 * held * steps * own_rows, held * SIDE * 4),
        name="describe",
    )(z, info)


def partial_kernel(steps, z_ref, line_ref, got_ref, terms_ref, *refs):
    outs, total_ref = refs[:steps], refs[steps]
    step = pl.program_id(0)
    total_rows = total_ref.shape[0]
    own_rows = total_rows // steps
    row, weight = line_ref[:1, :].astype(jnp.int32), line_ref[1:2, :]
    place = jnp.bitwise_and(row - z_ref[0] * own_rows, total_rows - 1)
    index = lax.broadcasted_iota(jnp.int32, (total_rows, row.shape[1]), 0)
    marks = jnp.where(index == place, weight, 0.0).astype(BF16)
    part = jnp.dot(marks, got_ref[...], preferred_element_type=F32)

    @pl.when(step == 0)
    def _():
        total_ref[...] = part

    @pl.when(step > 0)
    def _():
        total_ref[...] += part

    @pl.when(step == pl.num_programs(0) - 1)
    def _():
        for k in range(steps):
            outs[k][:own_rows, :] = total_ref[k * own_rows : (k + 1) * own_rows, :].astype(BF16)
            outs[k][own_rows:, :] = terms_ref[k * TAIL : (k + 1) * TAIL, :]


def partial_sums(z, lines, got, terms, steps, own_rows):
    held, width = got.shape
    some = held // 4
    return pl.pallas_call(
        functools.partial(partial_kernel, steps),
        grid=(held // some,),
        in_specs=[
            pl.BlockSpec(memory_space=pltpu.SMEM),
            pl.BlockSpec((HEAD, some), lambda g: (0, g)),
            pl.BlockSpec((some, width), lambda g: (g, 0)),
            pl.BlockSpec(terms.shape, lambda g: (0, 0)),
        ],
        out_specs=[pl.BlockSpec((own_rows + TAIL, width), lambda g: (0, 0))] * steps,
        out_shape=[jax.ShapeDtypeStruct((own_rows + TAIL, width), BF16)] * steps,
        scratch_shapes=[pltpu.VMEM((steps * own_rows, width), F32)],
        compiler_params=params(),
        cost_estimate=cost(2 * steps * own_rows * held * width, (held + steps * own_rows) * width * 2),
        name="partial_sums",
    )(z, lines, got, terms)


def average_kernel(own_rows, *refs):
    parts, out_ref = refs[:-1], refs[-1]
    terms = sum(ref[own_rows:, :].astype(F32) for ref in parts)
    line = jnp.sum(terms, axis=0, keepdims=True)
    below = jnp.maximum(jnp.broadcast_to(line, (SIDE, own_rows)).T, 1.0)
    total = sum(ref[:own_rows, :].astype(F32) for ref in parts)
    for k in range(total.shape[1] // SIDE):
        span = slice(k * SIDE, (k + 1) * SIDE)
        out_ref[:, span] = (total[:, span] / below).astype(BF16)


def average(parts, own_rows):
    width = parts[0].shape[1]
    vmem = pl.BlockSpec(memory_space=pltpu.VMEM)
    return pl.pallas_call(
        functools.partial(average_kernel, own_rows),
        in_specs=[vmem] * len(parts),
        out_specs=vmem,
        out_shape=jax.ShapeDtypeStruct((own_rows, width), BF16),
        compiler_params=params(),
        cost_estimate=cost(10 * own_rows * width, 18 * own_rows * width),
        name="average",
    )(*parts)


def subtract_kernel(count, sizes, line_ref, got_ref, coadd_ref, own_ref, out_ref):
    total_rows = coadd_ref.shape[0]
    sources = out_ref.shape[0]
    index = lax.broadcasted_iota(jnp.int32, (SIDE, total_rows), 1).astype(F32)
    marks = []
    for a in range(0, line_ref.shape[1], SIDE):
        column = jnp.broadcast_to(line_ref[:1, a : a + SIDE], (SIDE, SIDE)).T
        column = jnp.concatenate([column] * (total_rows // SIDE), axis=1)
        marks.append(jnp.where(index == column, 1.0, 0.0).astype(BF16))
    under = jnp.dot(jnp.concatenate(marks), coadd_ref[...], preferred_element_type=F32)
    diff = (got_ref[...].astype(F32) - under).astype(BF16)
    n_core, n_x, n_near, n_y = sizes
    for s in range(sources):
        out_ref[s, :count, :] = diff[s * count : (s + 1) * count]
        place = pl.program_id(0) * sources + s
        near = lax.rem(place // n_y, n_near)
        x = lax.rem(place // (n_y * n_near), n_x)
        core = place // (n_y * n_near * n_x)
        first = pl.multiple_of(((near * n_x + x) * n_core + core) * BLOCKS, BLOCKS)
        out_ref[s, count:, :] = own_ref[pl.ds(first, BLOCKS), :]


def subtract(lines, got, coadd, own, count, sizes):
    held, width = got.shape
    sources = held // count
    some = 16
    return pl.pallas_call(
        functools.partial(subtract_kernel, count, sizes),
        grid=(sources // some,),
        in_specs=[
            pl.BlockSpec((HEAD, some * count), lambda g: (0, g)),
            pl.BlockSpec((some * count, width), lambda g: (g, 0)),
            pl.BlockSpec(coadd.shape, lambda g: (0, 0)),
            pl.BlockSpec(own.shape, lambda g: (0, 0)),
        ],
        out_specs=pl.BlockSpec((some, count + BLOCKS, width), lambda g: (g, 0, 0)),
        out_shape=jax.ShapeDtypeStruct((sources, count + BLOCKS, width), BF16),
        compiler_params=params(),
        cost_estimate=cost(2 * coadd.shape[0] * held * width, (2 * held + coadd.shape[0]) * width * 2),
        name="subtract",
    )(lines, got, coadd, own)


def place_kernel(back_ref, coadd_ref, diff_ref, template_ref, m_ref):
    chunks, _, width = back_ref.shape
    per = width // SIDE
    for i in range(SIDE):
        t, k = divmod(i, per)
        m_ref[pl.ds(i, GROUP, stride=STRIDE), :] = back_ref[t, :, k * SIDE : (k + 1) * SIDE].astype(F32)
    for p in range(GROUP):
        diff_ref[p] = m_ref[p * STRIDE : p * STRIDE + SIDE, :].astype(BF16)
    for t in range(coadd_ref.shape[0]):
        template_ref[:, t * width : (t + 1) * width] = coadd_ref[t]


def place(back, count):
    chunks, _, width = back.shape
    steps = count // GROUP
    some = chunks // steps
    return pl.pallas_call(
        place_kernel,
        grid=(steps,),
        in_specs=[
            pl.BlockSpec((chunks, GROUP, width), lambda g: (0, g, 0)),
            pl.BlockSpec((some, BLOCKS, width), lambda g: (g, count // BLOCKS, 0)),
        ],
        out_specs=(
            pl.BlockSpec((GROUP, SIDE, SIDE), lambda g: (g, 0, 0)),
            pl.BlockSpec((BLOCKS, some * width), lambda g: (0, g)),
        ),
        out_shape=(
            jax.ShapeDtypeStruct((count, SIDE, SIDE), BF16),
            jax.ShapeDtypeStruct((BLOCKS, SIDE * SIDE), BF16),
        ),
        scratch_shapes=[pltpu.VMEM((GROUP * STRIDE, SIDE), F32)],
        compiler_params=params(),
        cost_estimate=cost(0, 4 * count * SIDE * SIDE),
        name="place",
    )(back, back)


def shift(array, by, steps):
    return lax.ppermute(array, FAR, [(i, (i + by) % steps) for i in range(steps)])


def body(pieces, row_taps, col_taps, coeffs, weights, blocks, routes):
    count = pieces.shape[0]
    steps = lax.axis_size(FAR)
    chunks = lax.axis_size(PLANE)
    own_rows = chunks // lax.axis_size("y") * BLOCKS
    sizes = tuple(lax.axis_size(name) for name in PLANE)
    z = lax.axis_index(FAR).astype(jnp.int32).reshape(1)
    others = sorted(range(1, steps), key=lambda k: -min(k, steps - k))

    row = jnp.pad((routes[:, 0] * BLOCKS + blocks).astype(F32), (0, SIDE - count))
    weight = jnp.pad(weights.astype(F32), (0, SIDE - count))
    line = lax.broadcasted_iota(jnp.int32, (chunks, HEAD, SIDE), 1)
    info = jnp.where(line == 0, row, weight)
    info = lax.all_to_all(info, PLANE, split_axis=0, concat_axis=0, tiled=True)

    sent = convolve(pieces, coeffs, col_taps, row_taps, chunks)
    got = lax.all_to_all(sent, PLANE, split_axis=0, concat_axis=0, tiled=True)
    got = got.reshape(chunks * count, -1)

    lines, terms = describe(z, info, steps, own_rows)
    sums = partial_sums(z, lines, got, terms, steps, own_rows)
    own = average([sums[0]] + [shift(sums[k], k, steps) for k in others], own_rows)
    coadd = lax.all_gather(own, FAR, axis=0, tiled=True)
    back = subtract(lines, got, coadd, own, count, sizes)
    back = lax.all_to_all(back, PLANE, split_axis=0, concat_axis=0, tiled=True)
    return place(back, count)


def solution(mesh):
    finer = Mesh(mesh.devices.reshape(4, 4, 2, 4, 2), EVERY)
    in_specs = (
        P(EVERY, None, None),
        P(),
        P(),
        P(EVERY, None),
        P(EVERY),
        P(EVERY),
        P(EVERY, None),
    )
    out_specs = (P(EVERY, None, None), P(EVERY[1:], None))
    return jax.shard_map(body, mesh=finer, in_specs=in_specs, out_specs=out_specs, check_vma=False)
```

```python
import functools

import jax
import jax.numpy as jnp
from jax import lax
from jax.experimental import pallas as pl
from jax.experimental.pallas import tpu as pltpu
from jax.sharding import Mesh, PartitionSpec as P

BLOCKS = 16
SIDE = 128
GROUP = 16
HEAD = 8
TAIL = 16
STRIDE = 132
FAR = "far"
PLANE = ("c", "x", "near", "y")
EVERY = ("y", "far", "near", "x", "c")
BF16 = jnp.bfloat16
F32 = jnp.float32


def params(limit=63 << 20):
    return pltpu.CompilerParams(vmem_limit_bytes=limit)


def cost(flops, nbytes):
    return pl.CostEstimate(flops=flops, bytes_accessed=nbytes, transcendentals=0)


def band(taps_ref, b, half):
    line = jnp.broadcast_to(taps_ref[b : b + 1, :], (SIDE, SIDE))
    moved = pltpu.roll(line, 0, 1, stride=1, stride_axis=0)
    rows = lax.broadcasted_iota(jnp.int32, (SIDE, SIDE), 0)
    columns = lax.broadcasted_iota(jnp.int32, (SIDE, SIDE), 1)
    return jnp.where(jnp.abs(columns - rows) <= half, moved, 0.0)


def conv_kernel(nb, half, coef_ref, x_ref, col_taps_ref, row_taps_ref, out_ref, col_ref, row_ref, taps_ref, z_ref, m_ref):
    step = pl.program_id(0)

    @pl.when(step == 0)
    def _():
        for source, target, flip in ((col_taps_ref, col_ref, True), (row_taps_ref, row_ref, False)):
            taps_ref[...] = jnp.zeros_like(taps_ref)
            taps_ref[:nb, : 2 * half + 1] = source[...].astype(F32)
            taps_ref[...] = pltpu.roll(taps_ref[...], SIDE - half, 1)
            for b in range(nb):
                matrix = band(taps_ref, b, half)
                matrix = matrix.T if flip else matrix
                target[:, b * SIDE : (b + 1) * SIDE] = matrix.astype(BF16)

    x = x_ref[...].reshape(GROUP * SIDE, SIDE)
    for first in range(0, nb, 2):
        some = min(2, nb - first)
        inner = jnp.dot(x, col_ref[:, first * SIDE : (first + some) * SIDE], preferred_element_type=F32)
        for k in range(some):
            b = first + k
            for p in range(GROUP):
                part = inner[p * SIDE : (p + 1) * SIDE, k * SIDE : (k + 1) * SIDE]
                z_ref[p // 2, b * SIDE : (b + 1) * SIDE, (p % 2) * SIDE : (p % 2 + 1) * SIDE] = (
                    part * coef_ref[step * GROUP + p, b]
                ).astype(BF16)
    for pair in range(GROUP // 2):
        outer = jnp.dot(row_ref[...], z_ref[pair], preferred_element_type=F32)
        for h in range(2):
            at = (2 * pair + h) * STRIDE
            m_ref[at : at + SIDE] = outer[:, h * SIDE : (h + 1) * SIDE]
    per = SIDE // out_ref.shape[0]
    for i in range(SIDE):
        t, k = divmod(i, per)
        out_ref[t, :, k * SIDE : (k + 1) * SIDE] = m_ref[pl.ds(i, GROUP, stride=STRIDE), :].astype(BF16)


def convolve(pieces, coeffs, col_taps, row_taps, chunks):
    count = pieces.shape[0]
    nb, width = row_taps.shape
    padded = -(-nb // 8) * 8
    return pl.pallas_call(
        functools.partial(conv_kernel, nb, (width - 1) // 2),
        grid=(count // GROUP,),
        in_specs=[
            pl.BlockSpec(memory_space=pltpu.SMEM),
            pl.BlockSpec((GROUP, SIDE, SIDE), lambda g: (g, 0, 0)),
            pl.BlockSpec((nb, width), lambda g: (0, 0)),
            pl.BlockSpec((nb, width), lambda g: (0, 0)),
        ],
        out_specs=pl.BlockSpec((chunks, GROUP, SIDE * SIDE // chunks), lambda g: (0, g, 0)),
        out_shape=jax.ShapeDtypeStruct((chunks, count, SIDE * SIDE // chunks), BF16),
        scratch_shapes=[
            pltpu.VMEM((SIDE, nb * SIDE), BF16),
            pltpu.VMEM((SIDE, nb * SIDE), BF16),
            pltpu.VMEM((padded, SIDE), F32),
            pltpu.VMEM((GROUP // 2, nb * SIDE, 2 * SIDE), BF16),
            pltpu.VMEM((GROUP * STRIDE, SIDE), F32),
        ],
        compiler_params=params(),
        cost_estimate=cost(count * nb * SIDE**3 * 4, count * SIDE * SIDE * 4),
        name="convolve",
    )(coeffs, pieces, col_taps, row_taps)


def describe_kernel(steps, own_rows, z_ref, info_ref, line_ref, out_ref):
    sources = info_ref.shape[0]
    left = lax.broadcasted_iota(jnp.int32, (1, SIDE), 1) < SIDE // 2
    for a in range(sources // 2):
        span = slice(a * SIDE, (a + 1) * SIDE)
        for line in range(2):
            even = info_ref[2 * a, line : line + 1, :]
            odd = pltpu.roll(info_ref[2 * a + 1, line : line + 1, :], SIDE // 2, 1)
            line_ref[line : line + 1, span] = jnp.where(left, even, odd)
    row, weight = line_ref[:1, :].astype(jnp.int32), line_ref[1:2, :]
    index = lax.broadcasted_iota(jnp.int32, (own_rows, row.shape[1]), 0)
    for k in range(steps):
        first = lax.rem(z_ref[0] + k, steps) * own_rows
        marks = jnp.where(index == row - first, weight, 0.0)
        total = jnp.broadcast_to(jnp.sum(marks, axis=1, keepdims=True), (own_rows, SIDE))
        total = total.T[:TAIL]
        high = total.astype(BF16).astype(F32)
        middle = (total - high).astype(BF16).astype(F32)
        low = total - high - middle
        line = lax.broadcasted_iota(jnp.int32, total.shape, 0)
        terms = jnp.where(line == 0, high, jnp.where(line == 1, middle, jnp.where(line == 2, low, 0.0)))
        out_ref[k * TAIL : (k + 1) * TAIL, :] = terms.astype(BF16)


def describe(z, info, steps, own_rows):
    held = info.shape[0] * SIDE // 2
    vmem = pl.BlockSpec(memory_space=pltpu.VMEM)
    return pl.pallas_call(
        functools.partial(describe_kernel, steps, own_rows),
        in_specs=[pl.BlockSpec(memory_space=pltpu.SMEM), vmem],
        out_specs=[vmem] * 2,
        out_shape=[jax.ShapeDtypeStruct((HEAD, held), F32)]
        + [jax.ShapeDtypeStruct((steps * TAIL, own_rows), BF16)],
        compiler_params=params(),
        cost_estimate=cost(4 * held * steps * own_rows, held * SIDE * 4),
        name="describe",
    )(z, info)


def partial_kernel(steps, z_ref, line_ref, got_ref, terms_ref, *outs):
    own_rows = outs[0].shape[0] - TAIL
    row, weight = line_ref[:1, :].astype(jnp.int32), line_ref[1:2, :]
    place = jnp.bitwise_and(row - z_ref[0] * own_rows, steps * own_rows - 1)
    index = lax.broadcasted_iota(jnp.int32, (own_rows, row.shape[1]), 0)
    for k in range(steps):
        marks = jnp.where(index + k * own_rows == place, weight, 0.0).astype(BF16)
        part = jnp.dot(marks, got_ref[...], preferred_element_type=F32)
        outs[k][:own_rows, :] = part.astype(BF16)
        outs[k][own_rows:, :] = terms_ref[k * TAIL : (k + 1) * TAIL, :]


def partial_sums(z, lines, got, terms, steps, own_rows):
    held, width = got.shape
    vmem = pl.BlockSpec(memory_space=pltpu.VMEM)
    return pl.pallas_call(
        functools.partial(partial_kernel, steps),
        in_specs=[pl.BlockSpec(memory_space=pltpu.SMEM)] + [vmem] * 3,
        out_specs=[vmem] * steps,
        out_shape=[jax.ShapeDtypeStruct((own_rows + TAIL, width), BF16)] * steps,
        compiler_params=params(),
        cost_estimate=cost(2 * steps * own_rows * held * width, (held + steps * own_rows) * width * 2),
        name="partial_sums",
    )(z, lines, got, terms)


def average_kernel(own_rows, *refs):
    parts, out_ref = refs[:-1], refs[-1]
    terms = sum(ref[own_rows:, :].astype(F32) for ref in parts)
    line = jnp.sum(terms, axis=0, keepdims=True)
    below = jnp.maximum(jnp.broadcast_to(line, (SIDE, own_rows)).T, 1.0)
    total = sum(ref[:own_rows, :].astype(F32) for ref in parts)
    for k in range(total.shape[1] // SIDE):
        span = slice(k * SIDE, (k + 1) * SIDE)
        out_ref[:, span] = (total[:, span] / below).astype(BF16)


def average(parts, own_rows):
    width = parts[0].shape[1]
    vmem = pl.BlockSpec(memory_space=pltpu.VMEM)
    return pl.pallas_call(
        functools.partial(average_kernel, own_rows),
        in_specs=[vmem] * len(parts),
        out_specs=vmem,
        out_shape=jax.ShapeDtypeStruct((own_rows, width), BF16),
        compiler_params=params(),
        cost_estimate=cost(10 * own_rows * width, 18 * own_rows * width),
        name="average",
    )(*parts)


def subtract_kernel(count, sizes, line_ref, got_ref, coadd_ref, own_ref, out_ref):
    total_rows = coadd_ref.shape[0]
    sources = out_ref.shape[0]
    index = lax.broadcasted_iota(jnp.int32, (SIDE, total_rows), 1).astype(F32)
    marks = []
    for a in range(0, line_ref.shape[1], SIDE):
        column = jnp.broadcast_to(line_ref[:1, a : a + SIDE], (SIDE, SIDE)).T
        column = jnp.concatenate([column] * (total_rows // SIDE), axis=1)
        marks.append(jnp.where(index == column, 1.0, 0.0).astype(BF16))
    under = jnp.dot(jnp.concatenate(marks), coadd_ref[...], preferred_element_type=F32)
    diff = (got_ref[...].astype(F32) - under).astype(BF16)
    n_core, n_x, n_near, n_y = sizes
    for s in range(sources):
        out_ref[s, :count, :] = diff[s * count : (s + 1) * count]
        place = pl.program_id(0) * sources + s
        near = lax.rem(place // n_y, n_near)
        x = lax.rem(place // (n_y * n_near), n_x)
        core = place // (n_y * n_near * n_x)
        first = pl.multiple_of(((near * n_x + x) * n_core + core) * BLOCKS, BLOCKS)
        out_ref[s, count:, :] = own_ref[pl.ds(first, BLOCKS), :]


def subtract(lines, got, coadd, own, count, sizes):
    held, width = got.shape
    sources = held // count
    some = 32
    return pl.pallas_call(
        functools.partial(subtract_kernel, count, sizes),
        grid=(sources // some,),
        in_specs=[
            pl.BlockSpec((HEAD, some * count), lambda g: (0, g)),
            pl.BlockSpec((some * count, width), lambda g: (g, 0)),
            pl.BlockSpec(coadd.shape, lambda g: (0, 0)),
            pl.BlockSpec(own.shape, lambda g: (0, 0)),
        ],
        out_specs=pl.BlockSpec((some, count + BLOCKS, width), lambda g: (g, 0, 0)),
        out_shape=jax.ShapeDtypeStruct((sources, count + BLOCKS, width), BF16),
        compiler_params=params(),
        cost_estimate=cost(2 * coadd.shape[0] * held * width, (2 * held + coadd.shape[0]) * width * 2),
        name="subtract",
    )(lines, got, coadd, own)


def place_kernel(back_ref, diff_ref, template_ref, here_ref, rows_ref, done_ref, flat_ref, m_ref, in_sems, out_sems):
    chunks, _, width = back_ref.shape
    per = width // SIDE
    steps = here_ref.shape[0]
    ins = [
        pltpu.make_async_copy(back_ref.at[:, pl.ds(g * GROUP, GROUP)], here_ref.at[g], in_sems.at[g]) for g in range(steps)
    ]
    ins.append(pltpu.make_async_copy(back_ref.at[:, pl.ds(steps * GROUP, BLOCKS)], rows_ref, in_sems.at[steps]))
    outs = [
        pltpu.make_async_copy(done_ref.at[pl.ds(g * GROUP, GROUP)], diff_ref.at[pl.ds(g * GROUP, GROUP)], out_sems.at[g])
        for g in range(steps)
    ]
    outs.append(pltpu.make_async_copy(flat_ref, template_ref, out_sems.at[steps]))
    for copy in ins:
        copy.start()
    for g in range(steps):
        ins[g].wait()
        for i in range(SIDE):
            t, k = divmod(i, per)
            m_ref[g % 2, pl.ds(i, GROUP, stride=STRIDE), :] = here_ref[g, t, :, k * SIDE : (k + 1) * SIDE].astype(F32)
        for p in range(GROUP):
            done_ref[g * GROUP + p] = m_ref[g % 2, p * STRIDE : p * STRIDE + SIDE, :].astype(BF16)
        outs[g].start()
    ins[steps].wait()
    for t in range(chunks):
        flat_ref[:, t * width : (t + 1) * width] = rows_ref[t]
    outs[steps].start()
    for copy in outs:
        copy.wait()


def place(back, count):
    chunks, _, width = back.shape
    steps = count // GROUP
    any_space = pl.BlockSpec(memory_space=pl.ANY)
    return pl.pallas_call(
        place_kernel,
        in_specs=[any_space],
        out_specs=[any_space, any_space],
        out_shape=[
            jax.ShapeDtypeStruct((count, SIDE, SIDE), BF16),
            jax.ShapeDtypeStruct((BLOCKS, SIDE * SIDE), BF16),
        ],
        scratch_shapes=[
            pltpu.VMEM((steps, chunks, GROUP, width), BF16),
            pltpu.VMEM((chunks, BLOCKS, width), BF16),
            pltpu.VMEM((count, SIDE, SIDE), BF16),
            pltpu.VMEM((BLOCKS, SIDE * SIDE), BF16),
            pltpu.VMEM((2, GROUP * STRIDE, SIDE), F32),
            pltpu.SemaphoreType.DMA((steps + 1,)),
            pltpu.SemaphoreType.DMA((steps + 1,)),
        ],
        compiler_params=params(),
        cost_estimate=cost(0, 4 * count * SIDE * SIDE),
        name="place",
    )(back)


def shift(array, by, steps):
    return lax.ppermute(array, FAR, [(i, (i + by) % steps) for i in range(steps)])


def body(pieces, row_taps, col_taps, coeffs, weights, blocks, routes):
    count = pieces.shape[0]
    steps = lax.axis_size(FAR)
    chunks = lax.axis_size(PLANE)
    own_rows = chunks // lax.axis_size("y") * BLOCKS
    sizes = tuple(lax.axis_size(name) for name in PLANE)
    z = lax.axis_index(FAR).astype(jnp.int32).reshape(1)
    others = sorted(range(1, steps), key=lambda k: -min(k, steps - k))

    row = jnp.pad((routes[:, 0] * BLOCKS + blocks).astype(F32), (0, SIDE - count))
    weight = jnp.pad(weights.astype(F32), (0, SIDE - count))
    line = lax.broadcasted_iota(jnp.int32, (chunks, HEAD, SIDE), 1)
    info = jnp.where(line == 0, row, weight)
    info = lax.all_to_all(info, PLANE, split_axis=0, concat_axis=0, tiled=True)

    sent = convolve(pieces, coeffs, col_taps, row_taps, chunks)
    got = lax.all_to_all(sent, PLANE, split_axis=0, concat_axis=0, tiled=True)
    got = got.reshape(chunks * count, -1)

    lines, terms = describe(z, info, steps, own_rows)
    sums = partial_sums(z, lines, got, terms, steps, own_rows)
    own = average([sums[0]] + [shift(sums[k], k, steps) for k in others], own_rows)
    coadd = lax.all_gather(own, FAR, axis=0, tiled=True)
    back = subtract(lines, got, coadd, own, count, sizes)
    back = lax.all_to_all(back, PLANE, split_axis=0, concat_axis=0, tiled=True)
    return place(back, count)


def solution(mesh):
    finer = Mesh(mesh.devices.reshape(4, 4, 2, 4, 2), EVERY)
    in_specs = (
        P(EVERY, None, None),
        P(),
        P(),
        P(EVERY, None),
        P(EVERY),
        P(EVERY),
        P(EVERY, None),
    )
    out_specs = (P(EVERY, None, None), P(EVERY[1:], None))
    return jax.shard_map(body, mesh=finer, in_specs=in_specs, out_specs=out_specs, check_vma=False)
```

```python
import functools

import jax
import jax.numpy as jnp
from jax import lax
from jax.experimental import pallas as pl
from jax.experimental.pallas import tpu as pltpu
from jax.sharding import Mesh, PartitionSpec as P

BLOCKS = 16
SIDE = 128
GROUP = 16
HEAD = 8
TAIL = 16
STRIDE = 132
FAR = "far"
PLANE = ("c", "x", "near", "y")
EVERY = ("y", "far", "near", "x", "c")
BF16 = jnp.bfloat16
F32 = jnp.float32


def params(limit=30 << 20):
    return pltpu.CompilerParams(vmem_limit_bytes=limit)


def cost(flops, nbytes):
    return pl.CostEstimate(flops=flops, bytes_accessed=nbytes, transcendentals=0)


def band(taps_ref, b, half):
    line = jnp.broadcast_to(taps_ref[b : b + 1, :], (SIDE, SIDE))
    moved = pltpu.roll(line, 0, 1, stride=1, stride_axis=0)
    rows = lax.broadcasted_iota(jnp.int32, (SIDE, SIDE), 0)
    columns = lax.broadcasted_iota(jnp.int32, (SIDE, SIDE), 1)
    return jnp.where(jnp.abs(columns - rows) <= half, moved, 0.0)


def conv_kernel(nb, half, coef_ref, x_ref, col_taps_ref, row_taps_ref, out_ref, col_ref, row_ref, taps_ref, z_ref, m_ref):
    step = pl.program_id(0)

    @pl.when(step == 0)
    def _():
        for source, target, flip in ((col_taps_ref, col_ref, True), (row_taps_ref, row_ref, False)):
            taps_ref[...] = jnp.zeros_like(taps_ref)
            taps_ref[:nb, : 2 * half + 1] = source[...].astype(F32)
            taps_ref[...] = pltpu.roll(taps_ref[...], SIDE - half, 1)
            for b in range(nb):
                matrix = band(taps_ref, b, half)
                matrix = matrix.T if flip else matrix
                target[:, b * SIDE : (b + 1) * SIDE] = matrix.astype(BF16)

    x = x_ref[...].reshape(GROUP * SIDE, SIDE)
    for first in range(0, nb, 2):
        some = min(2, nb - first)
        inner = jnp.dot(x, col_ref[:, first * SIDE : (first + some) * SIDE], preferred_element_type=F32)
        for k in range(some):
            b = first + k
            for p in range(GROUP):
                part = inner[p * SIDE : (p + 1) * SIDE, k * SIDE : (k + 1) * SIDE]
                z_ref[p // 2, b * SIDE : (b + 1) * SIDE, (p % 2) * SIDE : (p % 2 + 1) * SIDE] = (
                    part * coef_ref[step * GROUP + p, b]
                ).astype(BF16)
    for pair in range(GROUP // 2):
        outer = jnp.dot(row_ref[...], z_ref[pair], preferred_element_type=F32)
        for h in range(2):
            at = (2 * pair + h) * STRIDE
            m_ref[at : at + SIDE] = outer[:, h * SIDE : (h + 1) * SIDE]
    per = SIDE // out_ref.shape[0]
    for i in range(SIDE):
        t, k = divmod(i, per)
        out_ref[t, :, k * SIDE : (k + 1) * SIDE] = m_ref[pl.ds(i, GROUP, stride=STRIDE), :].astype(BF16)


def convolve(pieces, coeffs, col_taps, row_taps, chunks):
    count = pieces.shape[0]
    nb, width = row_taps.shape
    padded = -(-nb // 8) * 8
    return pl.pallas_call(
        functools.partial(conv_kernel, nb, (width - 1) // 2),
        grid=(count // GROUP,),
        in_specs=[
            pl.BlockSpec(memory_space=pltpu.SMEM),
            pl.BlockSpec((GROUP, SIDE, SIDE), lambda g: (g, 0, 0)),
            pl.BlockSpec((nb, width), lambda g: (0, 0)),
            pl.BlockSpec((nb, width), lambda g: (0, 0)),
        ],
        out_specs=pl.BlockSpec((chunks, GROUP, SIDE * SIDE // chunks), lambda g: (0, g, 0)),
        out_shape=jax.ShapeDtypeStruct((chunks, count, SIDE * SIDE // chunks), BF16),
        scratch_shapes=[
            pltpu.VMEM((SIDE, nb * SIDE), BF16),
            pltpu.VMEM((SIDE, nb * SIDE), BF16),
            pltpu.VMEM((padded, SIDE), F32),
            pltpu.VMEM((GROUP // 2, nb * SIDE, 2 * SIDE), BF16),
            pltpu.VMEM((GROUP * STRIDE, SIDE), F32),
        ],
        compiler_params=params(63 << 20),
        cost_estimate=cost(count * nb * SIDE**3 * 4, count * SIDE * SIDE * 4),
        name="convolve",
    )(coeffs, pieces, col_taps, row_taps)


def describe_kernel(steps, own_rows, z_ref, info_ref, line_ref, out_ref):
    sources = info_ref.shape[0]
    left = lax.broadcasted_iota(jnp.int32, (1, SIDE), 1) < SIDE // 2
    for a in range(sources // 2):
        span = slice(a * SIDE, (a + 1) * SIDE)
        for line in range(2):
            even = info_ref[2 * a, line : line + 1, :]
            odd = pltpu.roll(info_ref[2 * a + 1, line : line + 1, :], SIDE // 2, 1)
            line_ref[line : line + 1, span] = jnp.where(left, even, odd)
    row, weight = line_ref[:1, :].astype(jnp.int32), line_ref[1:2, :]
    index = lax.broadcasted_iota(jnp.int32, (own_rows, row.shape[1]), 0)
    for k in range(steps):
        first = lax.rem(z_ref[0] + k, steps) * own_rows
        marks = jnp.where(index == row - first, weight, 0.0)
        total = jnp.broadcast_to(jnp.sum(marks, axis=1, keepdims=True), (own_rows, SIDE))
        total = total.T[:TAIL]
        high = total.astype(BF16).astype(F32)
        middle = (total - high).astype(BF16).astype(F32)
        low = total - high - middle
        line = lax.broadcasted_iota(jnp.int32, total.shape, 0)
        terms = jnp.where(line == 0, high, jnp.where(line == 1, middle, jnp.where(line == 2, low, 0.0)))
        out_ref[k * TAIL : (k + 1) * TAIL, :] = terms.astype(BF16)


def describe(z, info, steps, own_rows):
    held = info.shape[0] * SIDE // 2
    vmem = pl.BlockSpec(memory_space=pltpu.VMEM)
    return pl.pallas_call(
        functools.partial(describe_kernel, steps, own_rows),
        in_specs=[pl.BlockSpec(memory_space=pltpu.SMEM), vmem],
        out_specs=[vmem] * 2,
        out_shape=[jax.ShapeDtypeStruct((HEAD, held), F32)]
        + [jax.ShapeDtypeStruct((steps * TAIL, own_rows), BF16)],
        compiler_params=params(),
        cost_estimate=cost(4 * held * steps * own_rows, held * SIDE * 4),
        name="describe",
    )(z, info)


def partial_kernel(steps, z_ref, line_ref, got_ref, terms_ref, *outs):
    own_rows = outs[0].shape[0] - TAIL
    row, weight = line_ref[:1, :].astype(jnp.int32), line_ref[1:2, :]
    place = jnp.bitwise_and(row - z_ref[0] * own_rows, steps * own_rows - 1)
    index = lax.broadcasted_iota(jnp.int32, (own_rows, row.shape[1]), 0)
    for k in range(steps):
        marks = jnp.where(index + k * own_rows == place, weight, 0.0).astype(BF16)
        part = jnp.dot(marks, got_ref[...], preferred_element_type=F32)
        outs[k][:own_rows, :] = part.astype(BF16)
        outs[k][own_rows:, :] = terms_ref[k * TAIL : (k + 1) * TAIL, :]


def partial_sums(z, lines, got, terms, steps, own_rows):
    held, width = got.shape
    vmem = pl.BlockSpec(memory_space=pltpu.VMEM)
    return pl.pallas_call(
        functools.partial(partial_kernel, steps),
        in_specs=[pl.BlockSpec(memory_space=pltpu.SMEM)] + [vmem] * 3,
        out_specs=[vmem] * steps,
        out_shape=[jax.ShapeDtypeStruct((own_rows + TAIL, width), BF16)] * steps,
        compiler_params=params(),
        cost_estimate=cost(2 * steps * own_rows * held * width, (held + steps * own_rows) * width * 2),
        name="partial_sums",
    )(z, lines, got, terms)


def average_kernel(own_rows, *refs):
    parts, out_ref = refs[:-1], refs[-1]
    terms = sum(ref[own_rows:, :].astype(F32) for ref in parts)
    line = jnp.sum(terms, axis=0, keepdims=True)
    below = jnp.maximum(jnp.broadcast_to(line, (SIDE, own_rows)).T, 1.0)
    total = sum(ref[:own_rows, :].astype(F32) for ref in parts)
    for k in range(total.shape[1] // SIDE):
        span = slice(k * SIDE, (k + 1) * SIDE)
        out_ref[:, span] = (total[:, span] / below).astype(BF16)


def average(parts, own_rows):
    width = parts[0].shape[1]
    vmem = pl.BlockSpec(memory_space=pltpu.VMEM)
    return pl.pallas_call(
        functools.partial(average_kernel, own_rows),
        in_specs=[vmem] * len(parts),
        out_specs=vmem,
        out_shape=jax.ShapeDtypeStruct((own_rows, width), BF16),
        compiler_params=params(),
        cost_estimate=cost(10 * own_rows * width, 18 * own_rows * width),
        name="average",
    )(*parts)


def subtract_kernel(count, sizes, line_ref, got_ref, coadd_ref, own_ref, out_ref):
    total_rows = coadd_ref.shape[0]
    sources = out_ref.shape[0]
    index = lax.broadcasted_iota(jnp.int32, (SIDE, total_rows), 1).astype(F32)
    marks = []
    for a in range(0, line_ref.shape[1], SIDE):
        column = jnp.broadcast_to(line_ref[:1, a : a + SIDE], (SIDE, SIDE)).T
        column = jnp.concatenate([column] * (total_rows // SIDE), axis=1)
        marks.append(jnp.where(index == column, 1.0, 0.0).astype(BF16))
    under = jnp.dot(jnp.concatenate(marks), coadd_ref[...], preferred_element_type=F32)
    diff = (got_ref[...].astype(F32) - under).astype(BF16)
    n_core, n_x, n_near, n_y = sizes
    for s in range(sources):
        out_ref[s, :count, :] = diff[s * count : (s + 1) * count]
        place = pl.program_id(0) * sources + s
        near = lax.rem(place // n_y, n_near)
        x = lax.rem(place // (n_y * n_near), n_x)
        core = place // (n_y * n_near * n_x)
        first = pl.multiple_of(((near * n_x + x) * n_core + core) * BLOCKS, BLOCKS)
        out_ref[s, count:, :] = own_ref[pl.ds(first, BLOCKS), :]


def subtract(lines, got, coadd, own, count, sizes):
    held, width = got.shape
    sources = held // count
    some = 64
    return pl.pallas_call(
        functools.partial(subtract_kernel, count, sizes),
        grid=(sources // some,),
        in_specs=[
            pl.BlockSpec((HEAD, some * count), lambda g: (0, g)),
            pl.BlockSpec((some * count, width), lambda g: (g, 0)),
            pl.BlockSpec(coadd.shape, lambda g: (0, 0)),
            pl.BlockSpec(own.shape, lambda g: (0, 0)),
        ],
        out_specs=pl.BlockSpec((some, count + BLOCKS, width), lambda g: (g, 0, 0)),
        out_shape=jax.ShapeDtypeStruct((sources, count + BLOCKS, width), BF16),
        compiler_params=params(),
        cost_estimate=cost(2 * coadd.shape[0] * held * width, (2 * held + coadd.shape[0]) * width * 2),
        name="subtract",
    )(lines, got, coadd, own)


def place_kernel(back_ref, diff_ref, template_ref, here_ref, rows_ref, done_ref, flat_ref, m_ref, in_sems, out_sems):
    chunks, _, width = back_ref.shape
    per = width // SIDE
    steps = here_ref.shape[0]
    ins = [
        pltpu.make_async_copy(back_ref.at[:, pl.ds(g * GROUP, GROUP)], here_ref.at[g], in_sems.at[g]) for g in range(steps)
    ]
    ins.append(pltpu.make_async_copy(back_ref.at[:, pl.ds(steps * GROUP, BLOCKS)], rows_ref, in_sems.at[steps]))
    outs = [
        pltpu.make_async_copy(done_ref.at[pl.ds(g * GROUP, GROUP)], diff_ref.at[pl.ds(g * GROUP, GROUP)], out_sems.at[g])
        for g in range(steps)
    ]
    outs.append(pltpu.make_async_copy(flat_ref, template_ref, out_sems.at[steps]))
    for copy in ins:
        copy.start()
    for g in range(steps):
        ins[g].wait()
        for i in range(SIDE):
            t, k = divmod(i, per)
            m_ref[g % 2, pl.ds(i, GROUP, stride=STRIDE), :] = here_ref[g, t, :, k * SIDE : (k + 1) * SIDE].astype(F32)
        for p in range(GROUP):
            done_ref[g * GROUP + p] = m_ref[g % 2, p * STRIDE : p * STRIDE + SIDE, :].astype(BF16)
        outs[g].start()
    ins[steps].wait()
    for t in range(chunks):
        flat_ref[:, t * width : (t + 1) * width] = rows_ref[t]
    outs[steps].start()
    for copy in outs:
        copy.wait()


def place(back, count):
    chunks, _, width = back.shape
    steps = count // GROUP
    any_space = pl.BlockSpec(memory_space=pl.ANY)
    return pl.pallas_call(
        place_kernel,
        in_specs=[any_space],
        out_specs=[any_space, any_space],
        out_shape=[
            jax.ShapeDtypeStruct((count, SIDE, SIDE), BF16),
            jax.ShapeDtypeStruct((BLOCKS, SIDE * SIDE), BF16),
        ],
        scratch_shapes=[
            pltpu.VMEM((steps, chunks, GROUP, width), BF16),
            pltpu.VMEM((chunks, BLOCKS, width), BF16),
            pltpu.VMEM((count, SIDE, SIDE), BF16),
            pltpu.VMEM((BLOCKS, SIDE * SIDE), BF16),
            pltpu.VMEM((2, GROUP * STRIDE, SIDE), F32),
            pltpu.SemaphoreType.DMA((steps + 1,)),
            pltpu.SemaphoreType.DMA((steps + 1,)),
        ],
        compiler_params=params(),
        cost_estimate=cost(0, 4 * count * SIDE * SIDE),
        name="place",
    )(back)


def shift(array, by, steps):
    return lax.ppermute(array, FAR, [(i, (i + by) % steps) for i in range(steps)])


def body(pieces, row_taps, col_taps, coeffs, weights, blocks, routes):
    count = pieces.shape[0]
    steps = lax.axis_size(FAR)
    chunks = lax.axis_size(PLANE)
    own_rows = chunks // lax.axis_size("y") * BLOCKS
    sizes = tuple(lax.axis_size(name) for name in PLANE)
    z = lax.axis_index(FAR).astype(jnp.int32).reshape(1)
    others = sorted(range(1, steps), key=lambda k: -min(k, steps - k))

    row = jnp.pad((routes[:, 0] * BLOCKS + blocks).astype(F32), (0, SIDE - count))
    weight = jnp.pad(weights.astype(F32), (0, SIDE - count))
    line = lax.broadcasted_iota(jnp.int32, (chunks, HEAD, SIDE), 1)
    info = jnp.where(line == 0, row, weight)
    info = lax.all_to_all(info, PLANE, split_axis=0, concat_axis=0, tiled=True)

    sent = convolve(pieces, coeffs, col_taps, row_taps, chunks)
    got = lax.all_to_all(sent, PLANE, split_axis=0, concat_axis=0, tiled=True)
    got = got.reshape(chunks * count, -1)

    lines, terms = describe(z, info, steps, own_rows)
    sums = partial_sums(z, lines, got, terms, steps, own_rows)
    own = average([sums[0]] + [shift(sums[k], k, steps) for k in others], own_rows)
    coadd = lax.all_gather(own, FAR, axis=0, tiled=True)
    back = subtract(lines, got, coadd, own, count, sizes)
    back = lax.all_to_all(back, PLANE, split_axis=0, concat_axis=0, tiled=True)
    return place(back, count)


def solution(mesh):
    finer = Mesh(mesh.devices.reshape(4, 4, 2, 4, 2), EVERY)
    in_specs = (
        P(EVERY, None, None),
        P(),
        P(),
        P(EVERY, None),
        P(EVERY),
        P(EVERY),
        P(EVERY, None),
    )
    out_specs = (P(EVERY, None, None), P(EVERY[1:], None))
    return jax.shard_map(body, mesh=finer, in_specs=in_specs, out_specs=out_specs, check_vma=False)
```

```python
import functools

import jax
import jax.numpy as jnp
from jax import lax
from jax.experimental import pallas as pl
from jax.experimental.pallas import tpu as pltpu
from jax.sharding import Mesh, PartitionSpec as P

BLOCKS = 16
SIDE = 128
GROUP = 16
HEAD = 8
TAIL = 16
STRIDE = 132
FAR = "far"
PLANE = ("c", "y", "x", "near")
EVERY = ("y", "far", "near", "x", "c")
BF16 = jnp.bfloat16
F32 = jnp.float32


def params(limit=30 << 20):
    return pltpu.CompilerParams(vmem_limit_bytes=limit)


def cost(flops, nbytes):
    return pl.CostEstimate(flops=flops, bytes_accessed=nbytes, transcendentals=0)


def band(taps_ref, b, half):
    line = jnp.broadcast_to(taps_ref[b : b + 1, :], (SIDE, SIDE))
    moved = pltpu.roll(line, 0, 1, stride=1, stride_axis=0)
    rows = lax.broadcasted_iota(jnp.int32, (SIDE, SIDE), 0)
    columns = lax.broadcasted_iota(jnp.int32, (SIDE, SIDE), 1)
    return jnp.where(jnp.abs(columns - rows) <= half, moved, 0.0)


def conv_kernel(nb, half, coeffs_ref, x_ref, col_taps_ref, row_taps_ref, out_ref, coef_ref, col_ref, row_ref, taps_ref, z_ref, m_ref, sem):
    step = pl.program_id(0)

    @pl.when(step == 0)
    def _():
        copy = pltpu.make_async_copy(coeffs_ref, coef_ref, sem)
        copy.start()
        for source, target, flip in ((col_taps_ref, col_ref, True), (row_taps_ref, row_ref, False)):
            taps_ref[...] = jnp.zeros_like(taps_ref)
            taps_ref[:nb, : 2 * half + 1] = source[...].astype(F32)
            taps_ref[...] = pltpu.roll(taps_ref[...], SIDE - half, 1)
            for b in range(nb):
                matrix = band(taps_ref, b, half)
                matrix = matrix.T if flip else matrix
                target[:, b * SIDE : (b + 1) * SIDE] = matrix.astype(BF16)
        copy.wait()

    x = x_ref[...].reshape(GROUP * SIDE, SIDE)
    for first in range(0, nb, 2):
        some = min(2, nb - first)
        inner = jnp.dot(x, col_ref[:, first * SIDE : (first + some) * SIDE], preferred_element_type=F32)
        for k in range(some):
            b = first + k
            for p in range(GROUP):
                part = inner[p * SIDE : (p + 1) * SIDE, k * SIDE : (k + 1) * SIDE]
                z_ref[p // 2, b * SIDE : (b + 1) * SIDE, (p % 2) * SIDE : (p % 2 + 1) * SIDE] = (
                    part * coef_ref[b, step * GROUP + p]
                ).astype(BF16)
    for pair in range(GROUP // 2):
        outer = jnp.dot(row_ref[...], z_ref[pair], preferred_element_type=F32)
        for h in range(2):
            at = (2 * pair + h) * STRIDE
            m_ref[at : at + SIDE] = outer[:, h * SIDE : (h + 1) * SIDE]
    per = SIDE // out_ref.shape[0]
    for i in range(SIDE):
        t, k = divmod(i, per)
        out_ref[t, :, k * SIDE : (k + 1) * SIDE] = m_ref[pl.ds(i, GROUP, stride=STRIDE), :].astype(BF16)


def convolve(pieces, coeffs, col_taps, row_taps, chunks):
    count = pieces.shape[0]
    nb, width = row_taps.shape
    padded = -(-nb // 8) * 8
    return pl.pallas_call(
        functools.partial(conv_kernel, nb, (width - 1) // 2),
        grid=(count // GROUP,),
        in_specs=[
            pl.BlockSpec(memory_space=pl.ANY),
            pl.BlockSpec((GROUP, SIDE, SIDE), lambda g: (g, 0, 0)),
            pl.BlockSpec((nb, width), lambda g: (0, 0)),
            pl.BlockSpec((nb, width), lambda g: (0, 0)),
        ],
        out_specs=pl.BlockSpec((chunks, GROUP, SIDE * SIDE // chunks), lambda g: (0, g, 0)),
        out_shape=jax.ShapeDtypeStruct((chunks, count, SIDE * SIDE // chunks), BF16),
        scratch_shapes=[
            pltpu.SMEM(coeffs.shape[::-1], F32),
            pltpu.VMEM((SIDE, nb * SIDE), BF16),
            pltpu.VMEM((SIDE, nb * SIDE), BF16),
            pltpu.VMEM((padded, SIDE), F32),
            pltpu.VMEM((GROUP // 2, nb * SIDE, 2 * SIDE), BF16),
            pltpu.VMEM((GROUP * STRIDE, SIDE), F32),
            pltpu.SemaphoreType.DMA(()),
        ],
        compiler_params=params(63 << 20),
        cost_estimate=cost(count * nb * SIDE**3 * 4, count * SIDE * SIDE * 4),
        name="convolve",
    )(coeffs.T, pieces, col_taps, row_taps)


def describe_kernel(steps, own_rows, z_ref, info_ref, line_ref, out_ref):
    sources = info_ref.shape[0]
    left = lax.broadcasted_iota(jnp.int32, (1, SIDE), 1) < SIDE // 2
    for a in range(sources // 2):
        span = slice(a * SIDE, (a + 1) * SIDE)
        for line in range(2):
            even = info_ref[2 * a, line : line + 1, :]
            odd = pltpu.roll(info_ref[2 * a + 1, line : line + 1, :], SIDE // 2, 1)
            line_ref[line : line + 1, span] = jnp.where(left, even, odd)
    row, weight = line_ref[:1, :].astype(jnp.int32), line_ref[1:2, :]
    index = lax.broadcasted_iota(jnp.int32, (own_rows, row.shape[1]), 0)
    for k in range(steps):
        first = lax.rem(z_ref[0] + k, steps) * own_rows
        marks = jnp.where(index == row - first, weight, 0.0)
        total = jnp.broadcast_to(jnp.sum(marks, axis=1, keepdims=True), (own_rows, SIDE))
        total = total.T[:TAIL]
        high = total.astype(BF16).astype(F32)
        middle = (total - high).astype(BF16).astype(F32)
        low = total - high - middle
        line = lax.broadcasted_iota(jnp.int32, total.shape, 0)
        terms = jnp.where(line == 0, high, jnp.where(line == 1, middle, jnp.where(line == 2, low, 0.0)))
        out_ref[k * TAIL : (k + 1) * TAIL, :] = terms.astype(BF16)


def describe(z, info, steps, own_rows):
    held = info.shape[0] * SIDE // 2
    vmem = pl.BlockSpec(memory_space=pltpu.VMEM)
    return pl.pallas_call(
        functools.partial(describe_kernel, steps, own_rows),
        in_specs=[pl.BlockSpec(memory_space=pltpu.SMEM), vmem],
        out_specs=[vmem] * 2,
        out_shape=[jax.ShapeDtypeStruct((HEAD, held), F32)]
        + [jax.ShapeDtypeStruct((steps * TAIL, own_rows), BF16)],
        compiler_params=params(),
        cost_estimate=cost(4 * held * steps * own_rows, held * SIDE * 4),
        name="describe",
    )(z, info)


def partial_kernel(steps, z_ref, line_ref, got_ref, terms_ref, *outs):
    own_rows = outs[0].shape[0] - TAIL
    row, weight = line_ref[:1, :].astype(jnp.int32), line_ref[1:2, :]
    place = jnp.bitwise_and(row - z_ref[0] * own_rows, steps * own_rows - 1)
    index = lax.broadcasted_iota(jnp.int32, (own_rows, row.shape[1]), 0)
    for k in range(steps):
        marks = jnp.where(index + k * own_rows == place, weight, 0.0).astype(BF16)
        part = jnp.dot(marks, got_ref[...], preferred_element_type=F32)
        outs[k][:own_rows, :] = part.astype(BF16)
        outs[k][own_rows:, :] = terms_ref[k * TAIL : (k + 1) * TAIL, :]


def partial_sums(z, lines, got, terms, steps, own_rows):
    held, width = got.shape
    vmem = pl.BlockSpec(memory_space=pltpu.VMEM)
    return pl.pallas_call(
        functools.partial(partial_kernel, steps),
        in_specs=[pl.BlockSpec(memory_space=pltpu.SMEM)] + [vmem] * 3,
        out_specs=[vmem] * steps,
        out_shape=[jax.ShapeDtypeStruct((own_rows + TAIL, width), BF16)] * steps,
        compiler_params=params(),
        cost_estimate=cost(2 * steps * own_rows * held * width, (held + steps * own_rows) * width * 2),
        name="partial_sums",
    )(z, lines, got, terms)


def average_kernel(own_rows, *refs):
    parts, out_ref = refs[:-1], refs[-1]
    terms = sum(ref[own_rows:, :].astype(F32) for ref in parts)
    line = jnp.sum(terms, axis=0, keepdims=True)
    below = jnp.maximum(jnp.broadcast_to(line, (SIDE, own_rows)).T, 1.0)
    total = sum(ref[:own_rows, :].astype(F32) for ref in parts)
    for k in range(total.shape[1] // SIDE):
        span = slice(k * SIDE, (k + 1) * SIDE)
        out_ref[:, span] = (total[:, span] / below).astype(BF16)


def average(parts, own_rows):
    width = parts[0].shape[1]
    vmem = pl.BlockSpec(memory_space=pltpu.VMEM)
    return pl.pallas_call(
        functools.partial(average_kernel, own_rows),
        in_specs=[vmem] * len(parts),
        out_specs=vmem,
        out_shape=jax.ShapeDtypeStruct((own_rows, width), BF16),
        compiler_params=params(),
        cost_estimate=cost(10 * own_rows * width, 18 * own_rows * width),
        name="average",
    )(*parts)


def subtract_kernel(count, sizes, line_ref, got_ref, coadd_ref, own_ref, out_ref):
    total_rows = coadd_ref.shape[0]
    sources = out_ref.shape[0]
    index = lax.broadcasted_iota(jnp.int32, (SIDE, total_rows), 1).astype(F32)
    marks = []
    for a in range(0, line_ref.shape[1], SIDE):
        column = jnp.broadcast_to(line_ref[:1, a : a + SIDE], (SIDE, SIDE)).T
        column = jnp.concatenate([column] * (total_rows // SIDE), axis=1)
        marks.append(jnp.where(index == column, 1.0, 0.0).astype(BF16))
    under = jnp.dot(jnp.concatenate(marks), coadd_ref[...], preferred_element_type=F32)
    diff = (got_ref[...].astype(F32) - under).astype(BF16)
    n_core, n_y, n_x, n_near = sizes
    for s in range(sources):
        out_ref[s, :count, :] = diff[s * count : (s + 1) * count]
        place = pl.program_id(0) * sources + s
        near = lax.rem(place, n_near)
        x = lax.rem(place // n_near, n_x)
        core = place // (n_near * n_x * n_y)
        first = pl.multiple_of(((near * n_x + x) * n_core + core) * BLOCKS, BLOCKS)
        out_ref[s, count:, :] = own_ref[pl.ds(first, BLOCKS), :]


def subtract(lines, got, coadd, own, count, sizes):
    held, width = got.shape
    sources = held // count
    some = 64
    return pl.pallas_call(
        functools.partial(subtract_kernel, count, sizes),
        grid=(sources // some,),
        in_specs=[
            pl.BlockSpec((HEAD, some * count), lambda g: (0, g)),
            pl.BlockSpec((some * count, width), lambda g: (g, 0)),
            pl.BlockSpec(coadd.shape, lambda g: (0, 0)),
            pl.BlockSpec(own.shape, lambda g: (0, 0)),
        ],
        out_specs=pl.BlockSpec((some, count + BLOCKS, width), lambda g: (g, 0, 0)),
        out_shape=jax.ShapeDtypeStruct((sources, count + BLOCKS, width), BF16),
        compiler_params=params(),
        cost_estimate=cost(2 * coadd.shape[0] * held * width, (2 * held + coadd.shape[0]) * width * 2),
        name="subtract",
    )(lines, got, coadd, own)


def place_kernel(back_ref, diff_ref, template_ref, here_ref, rows_ref, done_ref, flat_ref, m_ref, in_sems, out_sems):
    chunks, _, width = back_ref.shape
    per = width // SIDE
    steps = here_ref.shape[0]
    ins = [
        pltpu.make_async_copy(back_ref.at[:, pl.ds(g * GROUP, GROUP)], here_ref.at[g], in_sems.at[g]) for g in range(steps)
    ]
    ins.append(pltpu.make_async_copy(back_ref.at[:, pl.ds(steps * GROUP, BLOCKS)], rows_ref, in_sems.at[steps]))
    outs = [
        pltpu.make_async_copy(done_ref.at[pl.ds(g * GROUP, GROUP)], diff_ref.at[pl.ds(g * GROUP, GROUP)], out_sems.at[g])
        for g in range(steps)
    ]
    outs.append(pltpu.make_async_copy(flat_ref, template_ref, out_sems.at[steps]))
    for copy in ins:
        copy.start()
    for g in range(steps):
        ins[g].wait()
        for i in range(SIDE):
            t, k = divmod(i, per)
            m_ref[g % 2, pl.ds(i, GROUP, stride=STRIDE), :] = here_ref[g, t, :, k * SIDE : (k + 1) * SIDE].astype(F32)
        for p in range(GROUP):
            done_ref[g * GROUP + p] = m_ref[g % 2, p * STRIDE : p * STRIDE + SIDE, :].astype(BF16)
        outs[g].start()
    ins[steps].wait()
    for t in range(chunks):
        flat_ref[:, t * width : (t + 1) * width] = rows_ref[t]
    outs[steps].start()
    for copy in outs:
        copy.wait()


def place(back, count):
    chunks, _, width = back.shape
    steps = count // GROUP
    any_space = pl.BlockSpec(memory_space=pl.ANY)
    return pl.pallas_call(
        place_kernel,
        in_specs=[any_space],
        out_specs=[any_space, any_space],
        out_shape=[
            jax.ShapeDtypeStruct((count, SIDE, SIDE), BF16),
            jax.ShapeDtypeStruct((BLOCKS, SIDE * SIDE), BF16),
        ],
        scratch_shapes=[
            pltpu.VMEM((steps, chunks, GROUP, width), BF16),
            pltpu.VMEM((chunks, BLOCKS, width), BF16),
            pltpu.VMEM((count, SIDE, SIDE), BF16),
            pltpu.VMEM((BLOCKS, SIDE * SIDE), BF16),
            pltpu.VMEM((2, GROUP * STRIDE, SIDE), F32),
            pltpu.SemaphoreType.DMA((steps + 1,)),
            pltpu.SemaphoreType.DMA((steps + 1,)),
        ],
        compiler_params=params(),
        cost_estimate=cost(0, 4 * count * SIDE * SIDE),
        name="place",
    )(back)


def shift(array, by, steps):
    return lax.ppermute(array, FAR, [(i, (i + by) % steps) for i in range(steps)])


def body(pieces, row_taps, col_taps, coeffs, weights, blocks, routes):
    count = pieces.shape[0]
    steps = lax.axis_size(FAR)
    chunks = lax.axis_size(PLANE)
    own_rows = chunks // lax.axis_size("y") * BLOCKS
    sizes = tuple(lax.axis_size(name) for name in PLANE)
    z = lax.axis_index(FAR).astype(jnp.int32).reshape(1)
    others = sorted(range(1, steps), key=lambda k: -min(k, steps - k))

    row = jnp.pad((routes[:, 0] * BLOCKS + blocks).astype(F32), (0, SIDE - count))
    weight = jnp.pad(weights.astype(F32), (0, SIDE - count))
    line = lax.broadcasted_iota(jnp.int32, (chunks, HEAD, SIDE), 1)
    info = jnp.where(line == 0, row, weight)
    info = lax.all_to_all(info, PLANE, split_axis=0, concat_axis=0, tiled=True)

    sent = convolve(pieces, coeffs, col_taps, row_taps, chunks)
    got = lax.all_to_all(sent, PLANE, split_axis=0, concat_axis=0, tiled=True)
    got = got.reshape(chunks * count, -1)

    lines, terms = describe(z, info, steps, own_rows)
    sums = partial_sums(z, lines, got, terms, steps, own_rows)
    own = average([sums[0]] + [shift(sums[k], k, steps) for k in others], own_rows)
    coadd = lax.all_gather(own, FAR, axis=0, tiled=True)
    back = subtract(lines, got, coadd, own, count, sizes)
    back = lax.all_to_all(back, PLANE, split_axis=0, concat_axis=0, tiled=True)
    return place(back, count)


def solution(mesh):
    finer = Mesh(mesh.devices.reshape(4, 4, 2, 4, 2), EVERY)
    in_specs = (
        P(EVERY, None, None),
        P(),
        P(),
        P(EVERY, None),
        P(EVERY),
        P(EVERY),
        P(EVERY, None),
    )
    out_specs = (P(EVERY, None, None), P(EVERY[1:], None))
    return jax.shard_map(body, mesh=finer, in_specs=in_specs, out_specs=out_specs, check_vma=False)
```

```python
import functools

import jax
import jax.numpy as jnp
from jax import lax
from jax.experimental import pallas as pl
from jax.experimental.pallas import tpu as pltpu
from jax.sharding import Mesh, PartitionSpec as P

BLOCKS = 16
SIDE = 128
GROUP = 16
HEAD = 8
TAIL = 16
STRIDE = 132
FAR = "far"
PLANE = ("c", "y", "x", "near")
EVERY = ("y", "far", "near", "x", "c")
BF16 = jnp.bfloat16
F32 = jnp.float32


def params(limit=30 << 20):
    return pltpu.CompilerParams(vmem_limit_bytes=limit)


def cost(flops, nbytes):
    return pl.CostEstimate(flops=flops, bytes_accessed=nbytes, transcendentals=0)


def band(taps_ref, b, half):
    line = jnp.broadcast_to(taps_ref[b : b + 1, :], (SIDE, SIDE))
    moved = pltpu.roll(line, 0, 1, stride=1, stride_axis=0)
    rows = lax.broadcasted_iota(jnp.int32, (SIDE, SIDE), 0)
    columns = lax.broadcasted_iota(jnp.int32, (SIDE, SIDE), 1)
    return jnp.where(jnp.abs(columns - rows) <= half, moved, 0.0)


def conv_kernel(nb, half, coeffs_ref, x_ref, col_taps_ref, row_taps_ref, out_ref, coef_ref, col_ref, row_ref, taps_ref, z_ref, m_ref, sem):
    step = pl.program_id(0)

    @pl.when(step == 0)
    def _():
        copy = pltpu.make_async_copy(coeffs_ref, coef_ref, sem)
        copy.start()
        for source, target, flip in ((col_taps_ref, col_ref, True), (row_taps_ref, row_ref, False)):
            taps_ref[...] = jnp.zeros_like(taps_ref)
            taps_ref[:nb, : 2 * half + 1] = source[...].astype(F32)
            taps_ref[...] = pltpu.roll(taps_ref[...], SIDE - half, 1)
            for b in range(nb):
                matrix = band(taps_ref, b, half)
                matrix = matrix.T if flip else matrix
                target[:, b * SIDE : (b + 1) * SIDE] = matrix.astype(BF16)
        copy.wait()

    x = x_ref[...].reshape(GROUP * SIDE, SIDE)
    for first in range(0, nb, 2):
        some = min(2, nb - first)
        inner = jnp.dot(x, col_ref[:, first * SIDE : (first + some) * SIDE], preferred_element_type=F32)
        for k in range(some):
            b = first + k
            for p in range(GROUP):
                part = inner[p * SIDE : (p + 1) * SIDE, k * SIDE : (k + 1) * SIDE]
                z_ref[p // 2, b * SIDE : (b + 1) * SIDE, (p % 2) * SIDE : (p % 2 + 1) * SIDE] = (
                    part * coef_ref[b, step * GROUP + p]
                ).astype(BF16)
    for pair in range(GROUP // 2):
        outer = jnp.dot(row_ref[...], z_ref[pair], preferred_element_type=F32)
        for h in range(2):
            at = (2 * pair + h) * STRIDE
            m_ref[at : at + SIDE] = outer[:, h * SIDE : (h + 1) * SIDE]
    per = SIDE // out_ref.shape[0]
    for i in range(SIDE):
        t, k = divmod(i, per)
        out_ref[t, :, k * SIDE : (k + 1) * SIDE] = m_ref[pl.ds(i, GROUP, stride=STRIDE), :].astype(BF16)


def convolve(pieces, coeffs, col_taps, row_taps, chunks):
    count = pieces.shape[0]
    nb, width = row_taps.shape
    padded = -(-nb // 8) * 8
    return pl.pallas_call(
        functools.partial(conv_kernel, nb, (width - 1) // 2),
        grid=(count // GROUP,),
        in_specs=[
            pl.BlockSpec(memory_space=pl.ANY),
            pl.BlockSpec((GROUP, SIDE, SIDE), lambda g: (g, 0, 0)),
            pl.BlockSpec((nb, width), lambda g: (0, 0)),
            pl.BlockSpec((nb, width), lambda g: (0, 0)),
        ],
        out_specs=pl.BlockSpec((chunks, GROUP, SIDE * SIDE // chunks), lambda g: (0, g, 0)),
        out_shape=jax.ShapeDtypeStruct((chunks, count, SIDE * SIDE // chunks), BF16),
        scratch_shapes=[
            pltpu.SMEM(coeffs.shape[::-1], F32),
            pltpu.VMEM((SIDE, nb * SIDE), BF16),
            pltpu.VMEM((SIDE, nb * SIDE), BF16),
            pltpu.VMEM((padded, SIDE), F32),
            pltpu.VMEM((GROUP // 2, nb * SIDE, 2 * SIDE), BF16),
            pltpu.VMEM((GROUP * STRIDE, SIDE), F32),
            pltpu.SemaphoreType.DMA(()),
        ],
        compiler_params=params(63 << 20),
        cost_estimate=cost(count * nb * SIDE**3 * 4, count * SIDE * SIDE * 4),
        name="convolve",
    )(coeffs.T, pieces, col_taps, row_taps)


def lines_kernel(owner_ref, block_ref, weight_ref, out_ref, tile_ref):
    count = owner_ref.shape[1]
    tile_ref[...] = jnp.zeros_like(tile_ref)
    tile_ref[0:1, :count] = (owner_ref[...] * BLOCKS + block_ref[...]).astype(F32)
    tile_ref[1:2, :count] = weight_ref[...].astype(F32)
    out_ref[...] = jnp.broadcast_to(tile_ref[...][None], out_ref.shape)


def make_lines(routes, blocks, weights, chunks):
    count = blocks.shape[0]
    vmem = pl.BlockSpec(memory_space=pltpu.VMEM)
    return pl.pallas_call(
        lines_kernel,
        in_specs=[vmem] * 3,
        out_specs=vmem,
        out_shape=jax.ShapeDtypeStruct((chunks, HEAD, SIDE), F32),
        scratch_shapes=[pltpu.VMEM((HEAD, SIDE), F32)],
        compiler_params=params(63 << 20),
        cost_estimate=cost(0, chunks * HEAD * SIDE * 4),
        name="make_lines",
    )(routes.T, blocks.reshape(1, count), weights.reshape(1, count))


def describe_kernel(steps, own_rows, z_ref, info_ref, line_ref, out_ref):
    sources = info_ref.shape[0]
    left = lax.broadcasted_iota(jnp.int32, (1, SIDE), 1) < SIDE // 2
    for a in range(sources // 2):
        span = slice(a * SIDE, (a + 1) * SIDE)
        for line in range(2):
            even = info_ref[2 * a, line : line + 1, :]
            odd = pltpu.roll(info_ref[2 * a + 1, line : line + 1, :], SIDE // 2, 1)
            line_ref[line : line + 1, span] = jnp.where(left, even, odd)
    row, weight = line_ref[:1, :].astype(jnp.int32), line_ref[1:2, :]
    index = lax.broadcasted_iota(jnp.int32, (own_rows, row.shape[1]), 0)
    for k in range(steps):
        first = lax.rem(z_ref[0] + k, steps) * own_rows
        marks = jnp.where(index == row - first, weight, 0.0)
        total = jnp.broadcast_to(jnp.sum(marks, axis=1, keepdims=True), (own_rows, SIDE))
        total = total.T[:TAIL]
        high = total.astype(BF16).astype(F32)
        middle = (total - high).astype(BF16).astype(F32)
        low = total - high - middle
        line = lax.broadcasted_iota(jnp.int32, total.shape, 0)
        terms = jnp.where(line == 0, high, jnp.where(line == 1, middle, jnp.where(line == 2, low, 0.0)))
        out_ref[k * TAIL : (k + 1) * TAIL, :] = terms.astype(BF16)


def describe(z, info, steps, own_rows):
    held = info.shape[0] * SIDE // 2
    vmem = pl.BlockSpec(memory_space=pltpu.VMEM)
    return pl.pallas_call(
        functools.partial(describe_kernel, steps, own_rows),
        in_specs=[pl.BlockSpec(memory_space=pltpu.SMEM), vmem],
        out_specs=[vmem] * 2,
        out_shape=[jax.ShapeDtypeStruct((HEAD, held), F32)]
        + [jax.ShapeDtypeStruct((steps * TAIL, own_rows), BF16)],
        compiler_params=params(),
        cost_estimate=cost(4 * held * steps * own_rows, held * SIDE * 4),
        name="describe",
    )(z, info)


def partial_kernel(steps, z_ref, line_ref, got_ref, terms_ref, *outs):
    own_rows = outs[0].shape[0] - TAIL
    row, weight = line_ref[:1, :].astype(jnp.int32), line_ref[1:2, :]
    place = jnp.bitwise_and(row - z_ref[0] * own_rows, steps * own_rows - 1)
    index = lax.broadcasted_iota(jnp.int32, (own_rows, row.shape[1]), 0)
    for k in range(steps):
        marks = jnp.where(index + k * own_rows == place, weight, 0.0).astype(BF16)
        part = jnp.dot(marks, got_ref[...], preferred_element_type=F32)
        outs[k][:own_rows, :] = part.astype(BF16)
        outs[k][own_rows:, :] = terms_ref[k * TAIL : (k + 1) * TAIL, :]


def partial_sums(z, lines, got, terms, steps, own_rows):
    held, width = got.shape
    vmem = pl.BlockSpec(memory_space=pltpu.VMEM)
    return pl.pallas_call(
        functools.partial(partial_kernel, steps),
        in_specs=[pl.BlockSpec(memory_space=pltpu.SMEM)] + [vmem] * 3,
        out_specs=[vmem] * steps,
        out_shape=[jax.ShapeDtypeStruct((own_rows + TAIL, width), BF16)] * steps,
        compiler_params=params(),
        cost_estimate=cost(2 * steps * own_rows * held * width, (held + steps * own_rows) * width * 2),
        name="partial_sums",
    )(z, lines, got, terms)


def average_kernel(own_rows, *refs):
    parts, out_ref = refs[:-1], refs[-1]
    terms = sum(ref[own_rows:, :].astype(F32) for ref in parts)
    line = jnp.sum(terms, axis=0, keepdims=True)
    below = jnp.maximum(jnp.broadcast_to(line, (SIDE, own_rows)).T, 1.0)
    total = sum(ref[:own_rows, :].astype(F32) for ref in parts)
    for k in range(total.shape[1] // SIDE):
        span = slice(k * SIDE, (k + 1) * SIDE)
        out_ref[:, span] = (total[:, span] / below).astype(BF16)


def average(parts, own_rows):
    width = parts[0].shape[1]
    vmem = pl.BlockSpec(memory_space=pltpu.VMEM)
    return pl.pallas_call(
        functools.partial(average_kernel, own_rows),
        in_specs=[vmem] * len(parts),
        out_specs=vmem,
        out_shape=jax.ShapeDtypeStruct((own_rows, width), BF16),
        compiler_params=params(),
        cost_estimate=cost(10 * own_rows * width, 18 * own_rows * width),
        name="average",
    )(*parts)


def subtract_kernel(count, sizes, line_ref, got_ref, coadd_ref, own_ref, out_ref):
    total_rows = coadd_ref.shape[0]
    sources = out_ref.shape[0]
    index = lax.broadcasted_iota(jnp.int32, (SIDE, total_rows), 1).astype(F32)
    marks = []
    for a in range(0, line_ref.shape[1], SIDE):
        column = jnp.broadcast_to(line_ref[:1, a : a + SIDE], (SIDE, SIDE)).T
        column = jnp.concatenate([column] * (total_rows // SIDE), axis=1)
        marks.append(jnp.where(index == column, 1.0, 0.0).astype(BF16))
    under = jnp.dot(jnp.concatenate(marks), coadd_ref[...], preferred_element_type=F32)
    diff = (got_ref[...].astype(F32) - under).astype(BF16)
    n_core, n_y, n_x, n_near = sizes
    for s in range(sources):
        out_ref[s, :count, :] = diff[s * count : (s + 1) * count]
        place = pl.program_id(0) * sources + s
        near = lax.rem(place, n_near)
        x = lax.rem(place // n_near, n_x)
        core = place // (n_near * n_x * n_y)
        first = pl.multiple_of(((near * n_x + x) * n_core + core) * BLOCKS, BLOCKS)
        out_ref[s, count:, :] = own_ref[pl.ds(first, BLOCKS), :]


def subtract(lines, got, coadd, own, count, sizes):
    held, width = got.shape
    sources = held // count
    some = 64
    return pl.pallas_call(
        functools.partial(subtract_kernel, count, sizes),
        grid=(sources // some,),
        in_specs=[
            pl.BlockSpec((HEAD, some * count), lambda g: (0, g)),
            pl.BlockSpec((some * count, width), lambda g: (g, 0)),
            pl.BlockSpec(coadd.shape, lambda g: (0, 0)),
            pl.BlockSpec(own.shape, lambda g: (0, 0)),
        ],
        out_specs=pl.BlockSpec((some, count + BLOCKS, width), lambda g: (g, 0, 0)),
        out_shape=jax.ShapeDtypeStruct((sources, count + BLOCKS, width), BF16),
        compiler_params=params(),
        cost_estimate=cost(2 * coadd.shape[0] * held * width, (2 * held + coadd.shape[0]) * width * 2),
        name="subtract",
    )(lines, got, coadd, own)


def place_kernel(back_ref, diff_ref, template_ref, here_ref, rows_ref, done_ref, flat_ref, m_ref, in_sems, out_sems):
    chunks, _, width = back_ref.shape
    per = width // SIDE
    steps = here_ref.shape[0]
    ins = [
        pltpu.make_async_copy(back_ref.at[:, pl.ds(g * GROUP, GROUP)], here_ref.at[g], in_sems.at[g]) for g in range(steps)
    ]
    ins.append(pltpu.make_async_copy(back_ref.at[:, pl.ds(steps * GROUP, BLOCKS)], rows_ref, in_sems.at[steps]))
    outs = [
        pltpu.make_async_copy(done_ref.at[pl.ds(g * GROUP, GROUP)], diff_ref.at[pl.ds(g * GROUP, GROUP)], out_sems.at[g])
        for g in range(steps)
    ]
    outs.append(pltpu.make_async_copy(flat_ref, template_ref, out_sems.at[steps]))
    for copy in ins:
        copy.start()
    for g in range(steps):
        ins[g].wait()
        for i in range(SIDE):
            t, k = divmod(i, per)
            m_ref[g % 2, pl.ds(i, GROUP, stride=STRIDE), :] = here_ref[g, t, :, k * SIDE : (k + 1) * SIDE].astype(F32)
        for p in range(GROUP):
            done_ref[g * GROUP + p] = m_ref[g % 2, p * STRIDE : p * STRIDE + SIDE, :].astype(BF16)
        outs[g].start()
    ins[steps].wait()
    for t in range(chunks):
        flat_ref[:, t * width : (t + 1) * width] = rows_ref[t]
    outs[steps].start()
    for copy in outs:
        copy.wait()


def place(back, count):
    chunks, _, width = back.shape
    steps = count // GROUP
    any_space = pl.BlockSpec(memory_space=pl.ANY)
    return pl.pallas_call(
        place_kernel,
        in_specs=[any_space],
        out_specs=[any_space, any_space],
        out_shape=[
            jax.ShapeDtypeStruct((count, SIDE, SIDE), BF16),
            jax.ShapeDtypeStruct((BLOCKS, SIDE * SIDE), BF16),
        ],
        scratch_shapes=[
            pltpu.VMEM((steps, chunks, GROUP, width), BF16),
            pltpu.VMEM((chunks, BLOCKS, width), BF16),
            pltpu.VMEM((count, SIDE, SIDE), BF16),
            pltpu.VMEM((BLOCKS, SIDE * SIDE), BF16),
            pltpu.VMEM((2, GROUP * STRIDE, SIDE), F32),
            pltpu.SemaphoreType.DMA((steps + 1,)),
            pltpu.SemaphoreType.DMA((steps + 1,)),
        ],
        compiler_params=params(),
        cost_estimate=cost(0, 4 * count * SIDE * SIDE),
        name="place",
    )(back)


def shift(array, by, steps):
    return lax.ppermute(array, FAR, [(i, (i + by) % steps) for i in range(steps)])


def body(pieces, row_taps, col_taps, coeffs, weights, blocks, routes):
    count = pieces.shape[0]
    steps = lax.axis_size(FAR)
    chunks = lax.axis_size(PLANE)
    own_rows = chunks // lax.axis_size("y") * BLOCKS
    sizes = tuple(lax.axis_size(name) for name in PLANE)
    z = lax.axis_index(FAR).astype(jnp.int32).reshape(1)
    others = sorted(range(1, steps), key=lambda k: -min(k, steps - k))

    info = make_lines(routes, blocks, weights, chunks)
    info = lax.all_to_all(info, PLANE, split_axis=0, concat_axis=0, tiled=True)

    sent = convolve(pieces, coeffs, col_taps, row_taps, chunks)
    got = lax.all_to_all(sent, PLANE, split_axis=0, concat_axis=0, tiled=True)
    got = got.reshape(chunks * count, -1)

    lines, terms = describe(z, info, steps, own_rows)
    sums = partial_sums(z, lines, got, terms, steps, own_rows)
    own = average([sums[0]] + [shift(sums[k], k, steps) for k in others], own_rows)
    coadd = lax.all_gather(own, FAR, axis=0, tiled=True)
    back = subtract(lines, got, coadd, own, count, sizes)
    back = lax.all_to_all(back, PLANE, split_axis=0, concat_axis=0, tiled=True)
    return place(back, count)


def solution(mesh):
    finer = Mesh(mesh.devices.reshape(4, 4, 2, 4, 2), EVERY)
    in_specs = (
        P(EVERY, None, None),
        P(),
        P(),
        P(EVERY, None),
        P(EVERY),
        P(EVERY),
        P(EVERY, None),
    )
    out_specs = (P(EVERY, None, None), P(EVERY[1:], None))
    return jax.shard_map(body, mesh=finer, in_specs=in_specs, out_specs=out_specs, check_vma=False)
```
